128 devices in a mesh: tm: 16 (over z, x), rows: 8 (over y, core).
Axes of the slice: x: 4, y: 4, z: 4, core: 2. Of those that a mesh axis runs over, the one named last changes fastest.
Arguments:
- features: float32 [1048576, 512], P(('tm', 'rows'))
- response_lines: float32 [1048576, 128], P(('tm', 'rows'))
- row_counts: int32 [16], replicated, may hold values from 32768 to 65536, as said below
- ridge_codes: int32 [16], replicated, may hold values from 2 to 33
Outputs:
- forecast: bfloat16 [1048576, 128], P(('tm', 'rows'))
- partition_mse: float32 [16], P('tm')
The draws below stay inside these ranges and needn't reach their ends.
Inputs may be any that keep to these rules, and one draw needn't show every extreme that they name: `row_counts`: each count is a multiple of 128, at least half of 65536 and at most 65536.
All inputs are finite; a program needn't handle non-finite values.
Results may differ from the reference program's by a relative error of at most 0.001.
Values sent between devices are 32-bit elements; how exact they have to be, the bound alone decides.
A program may use at most 128 MiB of HBM per device.

```python
import math
import jax
import jax.numpy as jnp
from jax import lax

F = 512
RESPONSE_COUNT = 128
SHARD = 65536
OVERALL_LINES = 1048576
N_TM = 16


def joint_rows(key):
    base = jax.random.fold_in(key, 71)
    key_feat, key_coef, key_noise = jax.random.split(base, 3)
    feats = jax.random.normal(key_feat, (OVERALL_LINES, F), jnp.float32)
    coefs = jax.random.normal(key_coef, (F, RESPONSE_COUNT), jnp.float32) / math.sqrt(F)
    noise = 0.5 * jax.random.normal(key_noise, (OVERALL_LINES, RESPONSE_COUNT), jnp.float32)
    targs = jnp.dot(feats, coefs, precision=lax.Precision.HIGHEST) + noise
    return (feats, targs)


def draw_features(key, part):
    return joint_rows(key)[0]


def draw_response_lines(key, part):
    return joint_rows(key)[1]


def draw_row_counts(key, part):
    units = jax.random.randint(jax.random.fold_in(key, 13), (N_TM,), SHARD // 256, SHARD // 128 + 1)
    return (units * 128).astype(jnp.int32)


def place_ends(values, key, least, top_value):
    dims = values.shape
    spot = [jax.random.randint(jax.random.fold_in(key, axis), (), 0, dims[axis]) for axis in range(len(dims))]
    values = values.at[tuple(spot)].set(least)
    longest = dims.index(max(dims))
    spot[longest] = (spot[longest] + 1) % dims[longest]
    return values.at[tuple(spot)].set(top_value)


def setup_inputs(seed: int = 0) -> dict:
    seeds = jax.random.split(jax.random.key(seed), 5)
    return {
        "features": draw_features(jax.random.fold_in(seeds[4], 71), 0),
        "response_lines": draw_response_lines(jax.random.fold_in(seeds[4], 71), 0),
        "row_counts": draw_row_counts(jax.random.fold_in(seeds[4], 71), 0),
        "ridge_codes": place_ends(jax.random.randint(seeds[3], (N_TM,), 2, 34), jax.random.fold_in(seeds[3], 1), 2, 33).astype(jnp.int32),
    }


def ridge_solve(gram_sum, cross_sum, ridge_value):
    identity = jnp.eye(gram_sum.shape[0], dtype=jnp.float32)
    lower_factor = jnp.linalg.cholesky(gram_sum + ridge_value * identity)
    return jax.scipy.linalg.cho_solve((lower_factor, True), cross_sum)

def reference(features, response_lines, row_counts, ridge_codes):
    regressor_blocks = features.reshape(N_TM, SHARD, F)
    response_partitions = response_lines.reshape(N_TM, SHARD, RESPONSE_COUNT)
    positions = jnp.arange(SHARD, dtype=jnp.int32)
    usable_line_flags = (positions[None, :] < row_counts[:, None]).astype(jnp.float32)

    def shard_terms(packed_pair):
        feat_block, targ_block, valid_block = packed_pair
        weighted = feat_block * valid_block[:, None]
        gram_part = jnp.dot(weighted.T.astype(jnp.float32), feat_block.astype(jnp.float32), precision=lax.Precision.HIGHEST, preferred_element_type=jnp.float32)
        cross_part = jnp.dot(weighted.T.astype(jnp.float32), targ_block.astype(jnp.float32), precision=lax.Precision.HIGHEST, preferred_element_type=jnp.float32)
        return (gram_part, cross_part)
    gram_parts, cross_parts = lax.map(shard_terms, (regressor_blocks, response_partitions, usable_line_flags))
    gram_prefix = jnp.cumsum(gram_parts, axis=0)
    cross_prefix = jnp.cumsum(cross_parts, axis=0)
    seen = jnp.cumsum(row_counts.astype(jnp.float32))
    ridge_values = ridge_codes.astype(jnp.float32) * seen / 16.0

    def solve_single_anchor(packed_pair):
        return ridge_solve(packed_pair[0], packed_pair[1], packed_pair[2])
    weights = lax.map(solve_single_anchor, (gram_prefix, cross_prefix, ridge_values))
    prior_carry = jnp.concatenate([jnp.zeros((1, F, RESPONSE_COUNT), jnp.float32), weights[:-1]], axis=0)
    predicted_result = jnp.einsum('gbr,grd->gbd', regressor_blocks, prior_carry, precision=lax.Precision.HIGHEST) * usable_line_flags[:, :, None]
    residual_list = usable_line_flags[:, :, None] * (response_partitions - predicted_result) ** 2
    partition_mse = jnp.sum(residual_list, axis=(1, 2)) / (row_counts.astype(jnp.float32) * RESPONSE_COUNT)
    return (predicted_result.reshape(OVERALL_LINES, RESPONSE_COUNT).astype(jnp.bfloat16), partition_mse)
```

```python
import functools

import jax
import jax.numpy as jnp
from jax import lax
from jax.experimental import pallas as pl
from jax.experimental.pallas import tpu as pltpu
from jax.sharding import Mesh
from jax.sharding import PartitionSpec as P

TM = ("tm_0", "tm_1")
TM_ROWS = ("tm_0", "tm_1", "rows")
F32 = jnp.float32
BF = jnp.bfloat16
B = 128
WIDE = 16
MESH = pl.DeviceIdType.MESH


def halves_of(x):
    high = x.astype(BF)
    return high, (x - high.astype(F32)).astype(BF)


def thirds_of(x):
    high = x.astype(BF)
    left = x - high.astype(F32)
    middle = left.astype(BF)
    return high, middle, (left - middle.astype(F32)).astype(BF)


def mxu(left, right, dims=(1, 0)):
    contract = (((dims[0],), (dims[1],)), ((), ()))
    return lax.dot_general(left, right, contract, preferred_element_type=F32)


def full_dot(a, b, dims=(1, 0)):
    ah, am, al = thirds_of(a)
    bh, bm, bl = thirds_of(b)
    left = jnp.concatenate([ah, ah, am, am, ah, al], axis=dims[0])
    right = jnp.concatenate([bh, bm, bh, bm, bl, bh], axis=dims[1])
    return mxu(left, right, dims)


def gram_kernel(tile, valid_ref, x_ref, y_ref, out_ref, upper, lower, turned):
    step = pl.program_id(0)
    f, r = x_ref.shape[1], y_ref.shape[1]
    half = f // 2

    @pl.when(step == 0)
    def _():
        for acc in (upper, lower, turned):
            acc[...] = jnp.zeros_like(acc)

    rows = step * tile + lax.broadcasted_iota(jnp.int32, (tile, 1), 0)
    valid = rows < valid_ref[0]
    xh, xl = halves_of(jnp.where(valid, x_ref[...], 0.0))
    yh, yl = halves_of(y_ref[...])
    upper[...] += mxu(xh[:, :half], jnp.concatenate([yh, yl, xl, xh], axis=1), (0, 0))
    lower[...] += mxu(xh[:, half:], jnp.concatenate([yh, yl, xl, xh[:, half:]], axis=1), (0, 0))
    turned[...] += mxu(yh, xl, (0, 0))

    @pl.when(step == pl.num_programs(0) - 1)
    def _():
        def strip(i):
            acc = upper if i * B < half else lower
            return acc, pl.ds(i * B % half, B), 0 if i * B < half else half

        for i in range(f // B):
            a = pl.ds(i * B, B)
            acc, here, skipped = strip(i)
            for j in range(i, f // B):
                mirror, there, _ = strip(j)
                b = pl.ds(j * B, B)
                out_ref[a, b] = acc[here, pl.ds(2 * r + f + j * B - skipped, B)]
                out_ref[a, b] += acc[here, pl.ds(2 * r + j * B, B)]
                out_ref[a, b] += mirror[there, pl.ds(2 * r + i * B, B)].T
            out_ref[a, pl.ds(f, r)] = acc[here, pl.ds(0, r)] + acc[here, pl.ds(r, r)] + turned[:, a].T


def gram_and_cross(features, targets, valid):
    n, f = features.shape
    r = targets.shape[1]
    tile = 1024
    return pl.pallas_call(
        functools.partial(gram_kernel, tile),
        grid=(n // tile,),
        in_specs=[
            pl.BlockSpec(memory_space=pltpu.SMEM),
            pl.BlockSpec((tile, f), lambda i: (i, 0)),
            pl.BlockSpec((tile, r), lambda i: (i, 0)),
        ],
        out_specs=pl.BlockSpec((f, f + r), lambda i: (0, 0)),
        out_shape=jax.ShapeDtypeStruct((f, f + r), F32),
        scratch_shapes=[
            pltpu.VMEM((f // 2, 2 * f + 2 * r), F32),
            pltpu.VMEM((f // 2, 3 * f // 2 + 2 * r), F32),
            pltpu.VMEM((r, f), F32),
        ],
        compiler_params=pltpu.CompilerParams(vmem_limit_bytes=40 * 2**20),
        name="gram",
    )(valid, features, targets)


def row_of(x, s):
    return jnp.take_along_axis(x, jnp.full((8, B), s, jnp.int32), axis=0)


def column_of(x, c):
    return jnp.broadcast_to(x[:, c : c + 1], (8, B))


def negative_inverse(block):
    block = list(block)
    sub = lax.broadcasted_iota(jnp.int32, (8, B), 0)
    lane = lax.broadcasted_iota(jnp.int32, (8, B), 1)
    halves = WIDE // 8
    steps = B // WIDE
    for g in range(steps):
        mine = [halves * g + h for h in range(halves)]
        ahead = [halves * (g + 1) + h for h in range(halves)] if g + 1 < steps else []
        lo = WIDE * g
        inside = (lane >= lo) & (lane < lo + WIDE)
        cols = [[column_of(block[m], lo + c) for m in mine] for c in range(WIDE)]
        rows = jnp.concatenate([block[m] for m in mine], axis=0)
        right = [
            jnp.where(inside, jnp.where(lane - lo - 8 * h == sub, -1.0, 0.0), block[m])
            for h, m in enumerate(mine)
        ]
        later = {j: [column_of(block[j], lo + c) for c in range(WIDE)] for j in ahead}
        for p in range(WIDE // 2):
            r0, r1 = 2 * p, 2 * p + 1
            h, s0, s1 = r0 // 8, r0 % 8, r0 % 8 + 1
            a, b, c = row_of(cols[r0][h], s0), row_of(cols[r1][h], s0), row_of(cols[r1][h], s1)
            inverse = pl.reciprocal(a * c - b * b)
            at0, at1 = sub == s0, sub == s1
            both = at0 | at1
            n0, n1 = [], []
            for k in range(halves):
                x0 = cols[r0][k] * c - cols[r1][k] * b
                x1 = cols[r1][k] * a - cols[r0][k] * b
                if k == h:
                    x0 = jnp.where(at0, -c, jnp.where(at1, b, x0))
                    x1 = jnp.where(at0, b, jnp.where(at1, -a, x1))
                n0.append(x0)
                n1.append(x1)

            def swept(column):
                u, v = row_of(column[h], s0), row_of(column[h], s1)
                out = []
                for k in range(halves):
                    old = jnp.where(both, 0.0, column[k]) if k == h else column[k]
                    out.append(old - (n0[k] * u + n1[k] * v) * inverse)
                return out

            for q in range(r1 + 1, WIDE):
                cols[q] = swept(cols[q])
            right = swept(right)
        outer = full_dot(rows, jnp.concatenate(right, axis=0), (0, 0))
        terms = [row_of(right[c // 8], c % 8) for c in range(WIDE)] if ahead else None
        for j in range(B // 8):
            if j in mine:
                block[j] = right[j - mine[0]]
            elif j in ahead:
                value = jnp.where(inside, 0.0, block[j])
                for c in range(WIDE):
                    value = value - later[j][c] * terms[c]
                block[j] = value
            else:
                block[j] = jnp.where(inside, 0.0, block[j]) - outer[8 * j : 8 * j + 8, :]
    return jnp.concatenate(block, axis=0)


def solve_in_place(system, ridge):
    f, width = system.shape
    count = f // B
    diagonal = lax.broadcasted_iota(jnp.int32, (B, B), 0) == lax.broadcasted_iota(jnp.int32, (B, B), 1)
    for j in range(count):
        here = pl.ds(j * B, B)
        block = system[here, here] + jnp.where(diagonal, ridge, 0.0)
        inverse = negative_inverse([block[8 * i : 8 * i + 8, :] for i in range(B // 8)])
        rest = system[here, pl.ds((j + 1) * B, width - (j + 1) * B)]
        turned = full_dot(inverse, rest)
        system[here, pl.ds((j + 1) * B, width - (j + 1) * B)] = turned
        for k in range(j + 1, count):
            at = (k - j - 1) * B
            part = pl.ds(k * B, width - k * B)
            system[pl.ds(k * B, B), part] += full_dot(rest[:, at : at + B], turned[:, at:], (0, 0))
    last = pl.ds(f, width - f)
    for j in range(count - 2, -1, -1):
        here = pl.ds(j * B, B)
        behind = pl.ds((j + 1) * B, f - (j + 1) * B)
        system[here, last] += full_dot(system[here, behind], system[behind, last])


def fit_kernel(tile, valid_ref, ridge_ref, system_ref, x_hbm, y_hbm, out_ref, error_ref, system, x, y, sems):
    n, f = x.shape
    r = y.shape[1]
    get_x = pltpu.make_async_copy(x_hbm, x, sems.at[0])
    get_y = pltpu.make_async_copy(y_hbm, y, sems.at[1])
    get_x.start()
    get_y.start()
    for j in range(f // B):
        upper = (pl.ds(j * B, B), pl.ds(j * B, f + r - j * B))
        system[upper] = system_ref[upper]
    solve_in_place(system, ridge_ref[0])
    weights = -system[:, pl.ds(f, r)] * ridge_ref[1]
    wh, wl = halves_of(weights)
    both = jnp.concatenate([wh, wl], axis=1)
    get_x.wait()
    get_y.wait()
    error_ref[...] = jnp.zeros_like(error_ref)

    @pl.loop(0, n // tile)
    def _(i):
        here = pl.ds(pl.multiple_of(i * tile, tile), tile)
        xh, xl = halves_of(x[here, :])
        first = mxu(xh, both)
        value = first[:, :r] + first[:, r:] + mxu(xl, wh)
        valid = i * tile + lax.broadcasted_iota(jnp.int32, (tile, r), 0) < valid_ref[0]
        value = jnp.where(valid, value, 0.0)
        out_ref[here, :] = value.astype(BF)
        gap = jnp.where(valid, y[here, :] - value, 0.0)
        error_ref[...] += jnp.sum((gap * gap).reshape(tile // 8, 8, r), axis=0)


def fit_and_predict(system, features, targets, valid, ridge):
    n, f = features.shape
    r = targets.shape[1]
    smem, vmem = pl.BlockSpec(memory_space=pltpu.SMEM), pl.BlockSpec(memory_space=pltpu.VMEM)
    anywhere = pl.BlockSpec(memory_space=pl.ANY)
    return pl.pallas_call(
        functools.partial(fit_kernel, 512),
        in_specs=[smem, smem, vmem, anywhere, anywhere],
        out_specs=[vmem, vmem],
        out_shape=[jax.ShapeDtypeStruct((n, r), BF), jax.ShapeDtypeStruct((8, r), F32)],
        scratch_shapes=[
            pltpu.VMEM((f, f + r), F32),
            pltpu.VMEM((n, f), F32),
            pltpu.VMEM((n, r), F32),
            pltpu.SemaphoreType.DMA((2,)),
        ],
        compiler_params=pltpu.CompilerParams(vmem_limit_bytes=48 * 2**20),
        name="fit",
    )(valid, ridge, system, features, targets)


def prefix_kernel(part_ref, out_ref, twin_in, pair, row_in, mine, z_in, before, through, x_in, full, sends, arrivals):
    z, x, r = lax.axis_index("tm_0"), lax.axis_index("tm_1"), lax.axis_index("rows")
    y, core = r // 2, lax.rem(r, 2)
    twin = {"rows": r + 1 - 2 * core}
    f, width = part_ref.shape
    count, half, piece = f // B, B // 2, B // 8

    def other(i, d):
        return lax.rem(i + d, 4)

    barrier = pltpu.get_barrier_semaphore()
    pl.semaphore_signal(barrier, inc=1, device_id=twin, device_id_type=MESH)
    for d in (1, 2, 3):
        for peer in ({"rows": 2 * other(y, d) + core}, {"tm_0": other(z, d)}, {"tm_1": other(x, d)}):
            pl.semaphore_signal(barrier, inc=1, device_id=peer, device_id_type=MESH)
    pl.semaphore_wait(barrier, 10)

    def send(phase, j, d, src, dst, peer):
        at = (phase * count + j) * 3 + d - 1
        return pltpu.make_async_remote_copy(
            src_ref=src,
            dst_ref=dst,
            send_sem=sends.at[at],
            recv_sem=arrivals.at[at],
            device_id=peer,
            device_id_type=MESH,
        )

    def multiple(i):
        return pl.multiple_of(i, piece)

    def band(ref, j, start, size):
        return ref.at[pl.ds(multiple(j * B + start), size), pl.ds(j * B, width - j * B)]

    def small(ref, j, d=None):
        where = (pl.ds(j * piece, piece), pl.ds(j * B, width - j * B))
        return ref.at[where] if d is None else ref.at[(d - 1, *where)]

    def pair_rows(ref, j, start, size):
        return ref.at[pl.ds(multiple(j * half + start), size), pl.ds(j * B, width - j * B)]

    def to_twin(j):
        return send(0, j, 1, band(part_ref, j, half * (1 - core), half), pair_rows(twin_in, j, 0, half), twin)

    def to_row(j, d):
        to = other(y, d)
        return send(1, j, d, pair_rows(pair, j, piece * to, piece), small(row_in, j, d), {"rows": 2 * to + core})

    def to_z(j, d):
        return send(2, j, d, small(mine, j), small(z_in, j, d), {"tm_0": other(z, d)})

    def to_x(j, d, src):
        return send(3, j, d, small(src, j), small(x_in, j, d), {"tm_1": other(x, d)})

    def own(j):
        return band(full, j, half * core + piece * y, piece)

    def spread_row(j, d):
        return send(4, j, d, own(j), own(j), {"rows": 2 * other(y, d) + core})

    def row_arrival(j, d):
        there = band(full, j, half * core + piece * other(y, 4 - d), piece)
        return send(4, j, d, there, there, twin)

    def spread_twin(j):
        ours = band(full, j, half * core, half)
        return send(5, j, 1, ours, ours, twin)

    def twin_arrival(j):
        there = band(full, j, half * (1 - core), half)
        return send(5, j, 1, there, there, twin)

    def stage(p, j):
        if p == 0:
            to_twin(j).start()
        if p == 1:
            to_twin(j).wait_recv()
            pair_rows(pair, j, 0, half)[...] = (
                band(part_ref, j, half * core, half)[...] + pair_rows(twin_in, j, 0, half)[...]
            )
            for d in (1, 2, 3):
                to_row(j, d).start()
        if p == 2:
            total = pair_rows(pair, j, piece * y, piece)[...]
            for d in (1, 2, 3):
                to_row(j, d).wait_recv()
                total += small(row_in, j, d)[...]
            small(mine, j)[...] = total
            small(before, j)[...] = jnp.zeros_like(total)
            for d in (1, 2, 3):
                pl.when(z + d < 4)(lambda d=d: to_z(j, d).start())
        if p == 3:
            for d in (1, 2, 3):

                @pl.when(z >= d)
                def _(d=d):
                    to_z(j, d).wait_recv()
                    small(before, j)[...] += small(z_in, j, d)[...]

            small(through, j)[...] = small(before, j)[...] + small(mine, j)[...]
            for d in (1, 2, 3):
                pl.when(x + d < 4)(lambda d=d: to_x(j, d, through).start())
                pl.when(x + d >= 4)(lambda d=d: to_x(j, d, before).start())
        if p == 4:
            total = small(before, j)[...]
            for d in (1, 2, 3):
                to_x(j, d, before).wait_recv()
                total += small(x_in, j, d)[...]
            own(j)[...] = total
            for d in (1, 2, 3):
                spread_row(j, d).start()
        if p == 5:
            for d in (1, 2, 3):
                row_arrival(j, d).wait_recv()
            spread_twin(j).start()
        if p == 6:
            twin_arrival(j).wait_recv()
            band(out_ref, j, 0, B)[...] = band(full, j, 0, B)[...]

    for t in range(count + 6):
        for p in range(6, -1, -1):
            if 0 <= t - p < count:
                stage(p, t - p)
    for j in range(count):
        to_twin(j).wait_send()
        spread_twin(j).wait_send()
        for d in (1, 2, 3):
            to_row(j, d).wait_send()
            pl.when(z + d < 4)(lambda d=d: to_z(j, d).wait_send())
            to_x(j, d, before).wait_send()
            spread_row(j, d).wait_send()


def prefix_of_shards(part):
    f, width = part.shape
    count = f // B
    piece = (f // 8, width)
    return pl.pallas_call(
        prefix_kernel,
        in_specs=[pl.BlockSpec(memory_space=pltpu.VMEM)],
        out_specs=pl.BlockSpec(memory_space=pltpu.VMEM),
        out_shape=jax.ShapeDtypeStruct((f, width), F32),
        scratch_shapes=[
            pltpu.VMEM((f // 2, width), F32),
            pltpu.VMEM((f // 2, width), F32),
            pltpu.VMEM((3, *piece), F32),
            pltpu.VMEM(piece, F32),
            pltpu.VMEM((3, *piece), F32),
            pltpu.VMEM(piece, F32),
            pltpu.VMEM(piece, F32),
            pltpu.VMEM((3, *piece), F32),
            pltpu.VMEM((f, width), F32),
            pltpu.SemaphoreType.DMA((18 * count,)),
            pltpu.SemaphoreType.DMA((18 * count,)),
        ],
        compiler_params=pltpu.CompilerParams(
            collective_id=0, has_side_effects=True, vmem_limit_bytes=24 * 2**20
        ),
        name="prefix",
    )(part)


def body(features, targets, row_counts, ridge_codes):
    n = features.shape[0]
    shard = lax.axis_index(TM)
    counts = row_counts.astype(F32)
    valid = jnp.clip(row_counts[shard] - lax.axis_index("rows") * n, 0, n).reshape(1)
    system = gram_and_cross(features, targets, valid)
    system = prefix_of_shards(system)
    seen = jnp.sum(jnp.where(jnp.arange(counts.shape[0]) < shard, counts, 0.0))
    first = (shard == 0).astype(F32)
    ridge = ridge_codes[jnp.maximum(shard - 1, 0)].astype(F32) * seen / 16.0 + first
    forecast, errors = fit_and_predict(system, features, targets, valid, jnp.stack([ridge, 1.0 - first]))
    total = lax.psum(jnp.sum(errors), "rows")
    mse = total / (counts[shard] * targets.shape[1])
    return forecast, mse.reshape(1)


def solution(mesh):
    finer = Mesh(mesh.devices.reshape(4, 4, mesh.shape["rows"]), ("tm_0", "tm_1", "rows"))
    placed = (P(TM_ROWS, None), P(TM_ROWS, None), P(), P())
    return jax.shard_map(
        body, mesh=finer, in_specs=placed, out_specs=(P(TM_ROWS, None), P(TM)), check_vma=False
    )
```

```python
import functools

import jax
import jax.numpy as jnp
from jax import lax
from jax.experimental import pallas as pl
from jax.experimental.pallas import tpu as pltpu
from jax.sharding import Mesh
from jax.sharding import PartitionSpec as P

TM = ("tm_0", "tm_1")
TM_ROWS = ("tm_0", "tm_1", "rows")
F32 = jnp.float32
BF = jnp.bfloat16
B = 128
WIDE = 16
MESH = pl.DeviceIdType.MESH


def halves_of(x):
    high = x.astype(BF)
    return high, (x - high.astype(F32)).astype(BF)


def thirds_of(x):
    high = x.astype(BF)
    left = x - high.astype(F32)
    middle = left.astype(BF)
    return high, middle, (left - middle.astype(F32)).astype(BF)


def mxu(left, right, dims=(1, 0)):
    contract = (((dims[0],), (dims[1],)), ((), ()))
    return lax.dot_general(left, right, contract, preferred_element_type=F32)


def packed(i, j, f, width):
    return sum(width - k * B for k in range(i)) + (j - i) * B


def full_dot(a, b, dims=(1, 0)):
    ah, am, al = thirds_of(a)
    bh, bm, bl = thirds_of(b)
    left = jnp.concatenate([ah, ah, am, am, ah, al], axis=dims[0])
    right = jnp.concatenate([bh, bm, bh, bm, bl, bh], axis=dims[1])
    return mxu(left, right, dims)


def shard_index():
    return lax.axis_index("tm_0") * lax.axis_size("tm_1") + lax.axis_index("tm_1")


def valid_here(counts_ref, rows):
    return counts_ref[shard_index()] - lax.axis_index("rows") * rows


def gram_kernel(tile, counts_ref, x_ref, y_ref, out_ref, upper, lower, turned):
    step = pl.program_id(0)
    f, r = x_ref.shape[1], y_ref.shape[1]
    half = f // 2
    valid_rows = valid_here(counts_ref, tile * pl.num_programs(0))

    @pl.when(step == 0)
    def _():
        for acc in (upper, lower, turned):
            acc[...] = jnp.zeros_like(acc)

    rows = step * tile + lax.broadcasted_iota(jnp.int32, (tile, 1), 0)
    valid = rows < valid_rows
    xh, xl = halves_of(jnp.where(valid, x_ref[...], 0.0))
    yh, yl = halves_of(y_ref[...])
    upper[...] += mxu(xh[:, :half], jnp.concatenate([yh, yl, xl, xh], axis=1), (0, 0))
    lower[...] += mxu(xh[:, half:], jnp.concatenate([yh, yl, xl, xh[:, half:]], axis=1), (0, 0))
    turned[...] += mxu(yh, xl, (0, 0))

    @pl.when(step == pl.num_programs(0) - 1)
    def _():
        def strip(i):
            acc = upper if i * B < half else lower
            return acc, pl.ds(i * B % half, B), 0 if i * B < half else half

        for i in range(f // B):
            acc, here, skipped = strip(i)
            for j in range(i, f // B):
                mirror, there, _ = strip(j)
                b = pl.ds(packed(i, j, f, f + r), B)
                out_ref[:, b] = acc[here, pl.ds(2 * r + f + j * B - skipped, B)]
                out_ref[:, b] += acc[here, pl.ds(2 * r + j * B, B)]
                out_ref[:, b] += mirror[there, pl.ds(2 * r + i * B, B)].T
            b = pl.ds(packed(i, f // B, f, f + r), r)
            out_ref[:, b] = acc[here, pl.ds(0, r)]
            out_ref[:, b] += acc[here, pl.ds(r, r)]
            out_ref[:, b] += turned[:, pl.ds(i * B, B)].T


def gram_and_cross(features, targets, counts):
    n, f = features.shape
    r = targets.shape[1]
    tile = 1024
    columns = packed(f // B, f // B, f, f + r)
    return pl.pallas_call(
        functools.partial(gram_kernel, tile),
        grid=(n // tile,),
        in_specs=[
            pl.BlockSpec(memory_space=pltpu.SMEM),
            pl.BlockSpec((tile, f), lambda i: (i, 0)),
            pl.BlockSpec((tile, r), lambda i: (i, 0)),
        ],
        out_specs=pl.BlockSpec((B, columns), lambda i: (0, 0)),
        out_shape=jax.ShapeDtypeStruct((B, columns), F32),
        scratch_shapes=[
            pltpu.VMEM((f // 2, 2 * f + 2 * r), F32),
            pltpu.VMEM((f // 2, 3 * f // 2 + 2 * r), F32),
            pltpu.VMEM((r, f), F32),
        ],
        compiler_params=pltpu.CompilerParams(vmem_limit_bytes=56 * 2**20),
        name="gram",
    )(counts, features, targets)


def row_of(x, s):
    return jnp.take_along_axis(x, jnp.full((8, B), s, jnp.int32), axis=0)


def column_of(x, c):
    return jnp.broadcast_to(x[:, c : c + 1], (8, B))


def negative_inverse(block):
    block = list(block)
    sub = lax.broadcasted_iota(jnp.int32, (8, B), 0)
    lane = lax.broadcasted_iota(jnp.int32, (8, B), 1)
    halves = WIDE // 8
    steps = B // WIDE
    for g in range(steps):
        mine = [halves * g + h for h in range(halves)]
        ahead = [halves * (g + 1) + h for h in range(halves)] if g + 1 < steps else []
        lo = WIDE * g
        inside = (lane >= lo) & (lane < lo + WIDE)
        cols = [[column_of(block[m], lo + c) for m in mine] for c in range(WIDE)]
        rows = jnp.concatenate([block[m] for m in mine], axis=0)
        right = [
            jnp.where(inside, jnp.where(lane - lo - 8 * h == sub, -1.0, 0.0), block[m])
            for h, m in enumerate(mine)
        ]
        later = {j: [column_of(block[j], lo + c) for c in range(WIDE)] for j in ahead}
        for p in range(WIDE // 2):
            r0, r1 = 2 * p, 2 * p + 1
            h, s0, s1 = r0 // 8, r0 % 8, r0 % 8 + 1
            a, b, c = row_of(cols[r0][h], s0), row_of(cols[r1][h], s0), row_of(cols[r1][h], s1)
            inverse = pl.reciprocal(a * c - b * b)
            at0, at1 = sub == s0, sub == s1
            both = at0 | at1
            n0, n1 = [], []
            for k in range(halves):
                x0 = cols[r0][k] * c - cols[r1][k] * b
                x1 = cols[r1][k] * a - cols[r0][k] * b
                if k == h:
                    x0 = jnp.where(at0, -c, jnp.where(at1, b, x0))
                    x1 = jnp.where(at0, b, jnp.where(at1, -a, x1))
                n0.append(x0)
                n1.append(x1)

            def swept(column):
                u, v = row_of(column[h], s0), row_of(column[h], s1)
                out = []
                for k in range(halves):
                    old = jnp.where(both, 0.0, column[k]) if k == h else column[k]
                    out.append(old - (n0[k] * u + n1[k] * v) * inverse)
                return out

            for q in range(r1 + 1, WIDE):
                cols[q] = swept(cols[q])
            right = swept(right)
        outer = full_dot(rows, jnp.concatenate(right, axis=0), (0, 0))
        terms = [row_of(right[c // 8], c % 8) for c in range(WIDE)] if ahead else None
        for j in range(B // 8):
            if j in mine:
                block[j] = right[j - mine[0]]
            elif j in ahead:
                value = jnp.where(inside, 0.0, block[j])
                for c in range(WIDE):
                    value = value - later[j][c] * terms[c]
                block[j] = value
            else:
                block[j] = jnp.where(inside, 0.0, block[j]) - outer[8 * j : 8 * j + 8, :]
    return jnp.concatenate(block, axis=0)


def solve_in_place(system, ridge):
    f, width = system.shape
    count = f // B
    diagonal = lax.broadcasted_iota(jnp.int32, (B, B), 0) == lax.broadcasted_iota(jnp.int32, (B, B), 1)
    for j in range(count):
        here = pl.ds(j * B, B)
        block = system[here, here] + jnp.where(diagonal, ridge, 0.0)
        inverse = negative_inverse([block[8 * i : 8 * i + 8, :] for i in range(B // 8)])
        rest = system[here, pl.ds((j + 1) * B, width - (j + 1) * B)]
        turned = full_dot(inverse, rest)
        system[here, pl.ds((j + 1) * B, width - (j + 1) * B)] = turned
        for k in range(j + 1, count):
            at = (k - j - 1) * B
            part = pl.ds(k * B, width - k * B)
            system[pl.ds(k * B, B), part] += full_dot(rest[:, at : at + B], turned[:, at:], (0, 0))
    last = pl.ds(f, width - f)
    for j in range(count - 2, -1, -1):
        here = pl.ds(j * B, B)
        behind = pl.ds((j + 1) * B, f - (j + 1) * B)
        system[here, last] += full_dot(system[here, behind], system[behind, last])


def fit_kernel(tile, counts_ref, codes_ref, system_ref, x_hbm, y_hbm, out_ref, error_ref, system, x, y, sems):
    n, f = x.shape
    r = y.shape[1]
    get_x = pltpu.make_async_copy(x_hbm, x, sems.at[0])
    get_y = pltpu.make_async_copy(y_hbm, y, sems.at[1])
    get_x.start()
    get_y.start()
    for j in range(f // B):
        width = f + r - j * B
        system[pl.ds(j * B, B), pl.ds(j * B, width)] = system_ref[:, pl.ds(packed(j, j, f, f + r), width)]
    shard = shard_index()
    seen = jnp.int32(0)
    for k in range(counts_ref.shape[0]):
        seen += jnp.where(k < shard, counts_ref[k], 0)
    first = (shard == 0).astype(F32)
    ridge = codes_ref[jnp.maximum(shard - 1, 0)].astype(F32) * seen.astype(F32) * 0.0625 + first
    solve_in_place(system, ridge)
    weights = -system[:, pl.ds(f, r)] * (1.0 - first)
    valid_rows = valid_here(counts_ref, n)
    wh, wl = halves_of(weights)
    both = jnp.concatenate([wh, wl], axis=1)
    get_x.wait()
    get_y.wait()
    error_ref[...] = jnp.zeros_like(error_ref)

    @pl.loop(0, n // tile)
    def _(i):
        here = pl.ds(pl.multiple_of(i * tile, tile), tile)
        xh, xl = halves_of(x[here, :])
        first = mxu(xh, both)
        value = first[:, :r] + first[:, r:] + mxu(xl, wh)
        valid = i * tile + lax.broadcasted_iota(jnp.int32, (tile, r), 0) < valid_rows
        value = jnp.where(valid, value, 0.0)
        out_ref[here, :] = value.astype(BF)
        gap = jnp.where(valid, y[here, :] - value, 0.0)
        error_ref[...] += jnp.sum((gap * gap).reshape(tile // 8, 8, r), axis=0)


def fit_and_predict(system, features, targets, counts, codes):
    n, f = features.shape
    r = targets.shape[1]
    smem, vmem = pl.BlockSpec(memory_space=pltpu.SMEM), pl.BlockSpec(memory_space=pltpu.VMEM)
    anywhere = pl.BlockSpec(memory_space=pl.ANY)
    return pl.pallas_call(
        functools.partial(fit_kernel, 512),
        in_specs=[smem, smem, vmem, anywhere, anywhere],
        out_specs=[vmem, vmem],
        out_shape=[jax.ShapeDtypeStruct((n, r), BF), jax.ShapeDtypeStruct((8, r), F32)],
        scratch_shapes=[
            pltpu.VMEM((f, f + r), F32),
            pltpu.VMEM((n, f), F32),
            pltpu.VMEM((n, r), F32),
            pltpu.SemaphoreType.DMA((2,)),
        ],
        compiler_params=pltpu.CompilerParams(vmem_limit_bytes=56 * 2**20),
        name="fit",
    )(counts, codes, system, features, targets)


def prefix_kernel(chunks, part_ref, out_ref, twin_in, pair, row_in, mine, z_in, before, through, x_in, full, sends, arrivals):
    z, x, r = lax.axis_index("tm_0"), lax.axis_index("tm_1"), lax.axis_index("rows")
    y, core = r // 2, lax.rem(r, 2)
    twin = {"rows": r + 1 - 2 * core}
    count, half, piece = len(chunks), B // 2, B // 8

    def other(i, d):
        return lax.rem(i + d, 4)

    barrier = pltpu.get_barrier_semaphore()
    pl.semaphore_signal(barrier, inc=1, device_id=twin, device_id_type=MESH)
    for d in (1, 2, 3):
        for peer in ({"rows": 2 * other(y, d) + core}, {"tm_0": other(z, d)}, {"tm_1": other(x, d)}):
            pl.semaphore_signal(barrier, inc=1, device_id=peer, device_id_type=MESH)
    pl.semaphore_wait(barrier, 10)

    def send(phase, j, d, src, dst, peer):
        at = (phase * count + j) * 3 + d - 1
        return pltpu.make_async_remote_copy(
            src_ref=src,
            dst_ref=dst,
            send_sem=sends.at[at],
            recv_sem=arrivals.at[at],
            device_id=peer,
            device_id_type=MESH,
        )

    def multiple(i):
        return pl.multiple_of(i, piece)

    def part(ref, j, start, size, d=None):
        rows = pl.ds(start if isinstance(start, int) else multiple(start), size)
        where = (rows, pl.ds(*chunks[j]))
        return ref.at[where] if d is None else ref.at[(d - 1, *where)]

    def small(ref, j, d=None):
        return part(ref, j, 0, piece, d)

    def to_twin(j):
        return send(0, j, 1, part(part_ref, j, half * (1 - core), half), part(twin_in, j, 0, half), twin)

    def to_row(j, d):
        to = other(y, d)
        return send(1, j, d, part(pair, j, piece * to, piece), small(row_in, j, d), {"rows": 2 * to + core})

    def to_z(j, d):
        return send(2, j, d, small(mine, j), small(z_in, j, d), {"tm_0": other(z, d)})

    def to_x(j, d, src):
        return send(3, j, d, small(src, j), small(x_in, j, d), {"tm_1": other(x, d)})

    def own(j):
        return part(full, j, half * core + piece * y, piece)

    def spread_row(j, d):
        return send(4, j, d, own(j), own(j), {"rows": 2 * other(y, d) + core})

    def row_arrival(j, d):
        there = part(full, j, half * core + piece * other(y, 4 - d), piece)
        return send(4, j, d, there, there, twin)

    def spread_twin(j):
        ours = part(full, j, half * core, half)
        return send(5, j, 1, ours, ours, twin)

    def twin_arrival(j):
        there = part(full, j, half * (1 - core), half)
        return send(5, j, 1, there, there, twin)

    def stage(p, j):
        if p == 0:
            to_twin(j).start()
        if p == 1:
            to_twin(j).wait_recv()
            part(pair, j, 0, half)[...] = (
                part(part_ref, j, half * core, half)[...] + part(twin_in, j, 0, half)[...]
            )
            for d in (1, 2, 3):
                to_row(j, d).start()
        if p == 2:
            total = part(pair, j, piece * y, piece)[...]
            for d in (1, 2, 3):
                to_row(j, d).wait_recv()
                total += small(row_in, j, d)[...]
            small(mine, j)[...] = total
            small(before, j)[...] = jnp.zeros_like(total)
            for d in (1, 2, 3):
                pl.when(z + d < 4)(lambda d=d: to_z(j, d).start())
        if p == 3:
            for d in (1, 2, 3):

                @pl.when(z >= d)
                def _(d=d):
                    to_z(j, d).wait_recv()
                    small(before, j)[...] += small(z_in, j, d)[...]

            small(through, j)[...] = small(before, j)[...] + small(mine, j)[...]
            for d in (1, 2, 3):
                pl.when(x + d < 4)(lambda d=d: to_x(j, d, through).start())
                pl.when(x + d >= 4)(lambda d=d: to_x(j, d, before).start())
        if p == 4:
            total = small(before, j)[...]
            for d in (1, 2, 3):
                to_x(j, d, before).wait_recv()
                total += small(x_in, j, d)[...]
            own(j)[...] = total
            for d in (1, 2, 3):
                spread_row(j, d).start()
        if p == 5:
            for d in (1, 2, 3):
                row_arrival(j, d).wait_recv()
            spread_twin(j).start()
        if p == 6:
            twin_arrival(j).wait_recv()
            part(out_ref, j, 0, B)[...] = part(full, j, 0, B)[...]

    for t in range(count + 6):
        for p in range(6, -1, -1):
            if 0 <= t - p < count:
                stage(p, t - p)
    for j in range(count):
        to_twin(j).wait_send()
        spread_twin(j).wait_send()
        for d in (1, 2, 3):
            to_row(j, d).wait_send()
            pl.when(z + d < 4)(lambda d=d: to_z(j, d).wait_send())
            to_x(j, d, before).wait_send()
            spread_row(j, d).wait_send()


CHUNKS = (640, 1152)


def prefix_of_shards(value):
    columns = value.shape[1]
    chunks = [(sum(CHUNKS[:k]), w) for k, w in enumerate(CHUNKS)]
    half, piece = (B // 2, columns), (B // 8, columns)
    count = len(chunks)
    return pl.pallas_call(
        functools.partial(prefix_kernel, chunks),
        in_specs=[pl.BlockSpec(memory_space=pltpu.VMEM)],
        out_specs=pl.BlockSpec(memory_space=pltpu.VMEM),
        out_shape=jax.ShapeDtypeStruct((B, columns), F32),
        scratch_shapes=[
            pltpu.VMEM(half, F32),
            pltpu.VMEM(half, F32),
            pltpu.VMEM((3, *piece), F32),
            pltpu.VMEM(piece, F32),
            pltpu.VMEM((3, *piece), F32),
            pltpu.VMEM(piece, F32),
            pltpu.VMEM(piece, F32),
            pltpu.VMEM((3, *piece), F32),
            pltpu.VMEM((B, columns), F32),
            pltpu.SemaphoreType.DMA((18 * count,)),
            pltpu.SemaphoreType.DMA((18 * count,)),
        ],
        compiler_params=pltpu.CompilerParams(
            collective_id=0, has_side_effects=True, vmem_limit_bytes=24 * 2**20
        ),
        name="prefix",
    )(value)


def error_kernel(targets, counts_ref, error_ref, out_ref, gathered, sends, arrivals):
    r = lax.axis_index("rows")
    size = lax.axis_size("rows")

    def peer(d):
        return {"rows": lax.rem(r + d, size)}

    barrier = pltpu.get_barrier_semaphore()
    for d in range(1, size):
        pl.semaphore_signal(barrier, inc=1, device_id=peer(d), device_id_type=MESH)
    pl.semaphore_wait(barrier, size - 1)
    copies = [
        pltpu.make_async_remote_copy(
            src_ref=error_ref,
            dst_ref=gathered.at[d - 1],
            send_sem=sends.at[d - 1],
            recv_sem=arrivals.at[d - 1],
            device_id=peer(d),
            device_id_type=MESH,
        )
        for d in range(1, size)
    ]
    for copy in copies:
        copy.start()
    total = error_ref[...]
    for d, copy in enumerate(copies):
        copy.wait_recv()
        total += gathered[d]
    out_ref[0] = jnp.sum(total) / (counts_ref[shard_index()].astype(F32) * targets)
    for copy in copies:
        copy.wait_send()


def mean_error(errors, counts, targets):
    size = lax.axis_size("rows")
    smem, vmem = pl.BlockSpec(memory_space=pltpu.SMEM), pl.BlockSpec(memory_space=pltpu.VMEM)
    return pl.pallas_call(
        functools.partial(error_kernel, targets),
        in_specs=[smem, vmem],
        out_specs=smem,
        out_shape=jax.ShapeDtypeStruct((1,), F32),
        scratch_shapes=[
            pltpu.VMEM((size - 1, *errors.shape), F32),
            pltpu.SemaphoreType.DMA((size - 1,)),
            pltpu.SemaphoreType.DMA((size - 1,)),
        ],
        compiler_params=pltpu.CompilerParams(collective_id=1, has_side_effects=True),
        name="error",
    )(counts, errors)


def body(features, targets, row_counts, ridge_codes):
    system = prefix_of_shards(gram_and_cross(features, targets, row_counts))
    forecast, errors = fit_and_predict(system, features, targets, row_counts, ridge_codes)
    return forecast, mean_error(errors, row_counts, targets.shape[1])


def solution(mesh):
    finer = Mesh(mesh.devices.reshape(4, 4, mesh.shape["rows"]), ("tm_0", "tm_1", "rows"))
    placed = (P(TM_ROWS, None), P(TM_ROWS, None), P(), P())
    return jax.shard_map(
        body, mesh=finer, in_specs=placed, out_specs=(P(TM_ROWS, None), P(TM)), check_vma=False
    )
```

```python
import functools

import jax
import jax.numpy as jnp
from jax import lax
from jax.experimental import pallas as pl
from jax.experimental.pallas import tpu as pltpu
from jax.sharding import Mesh
from jax.sharding import PartitionSpec as P

TM = ("tm_0", "tm_1")
TM_ROWS = ("tm_0", "tm_1", "rows")
F32 = jnp.float32
BF = jnp.bfloat16
B = 128
WIDE = 16
MESH = pl.DeviceIdType.MESH


def halves_of(x):
    high = x.astype(BF)
    return high, (x - high.astype(F32)).astype(BF)


def thirds_of(x):
    high = x.astype(BF)
    left = x - high.astype(F32)
    middle = left.astype(BF)
    return high, middle, (left - middle.astype(F32)).astype(BF)


def mxu(left, right, dims=(1, 0)):
    contract = (((dims[0],), (dims[1],)), ((), ()))
    return lax.dot_general(left, right, contract, preferred_element_type=F32)


def packed(i, j, f, width):
    return sum(width - k * B for k in range(i)) + (j - i) * B


def full_dot(a, b, dims=(1, 0)):
    ah, am, al = thirds_of(a)
    bh, bm, bl = thirds_of(b)
    left = jnp.concatenate([ah, ah, am, am, ah, al], axis=dims[0])
    right = jnp.concatenate([bh, bm, bh, bm, bl, bh], axis=dims[1])
    return mxu(left, right, dims)


def shard_index():
    return lax.axis_index("tm_0") * lax.axis_size("tm_1") + lax.axis_index("tm_1")


def valid_here(counts_ref, rows):
    return counts_ref[shard_index()] - lax.axis_index("rows") * rows


def row_of(x, s):
    return jnp.take_along_axis(x, jnp.full((8, B), s, jnp.int32), axis=0)


def column_of(x, c):
    return jnp.broadcast_to(x[:, c : c + 1], (8, B))


def negative_inverse(block):
    block = list(block)
    sub = lax.broadcasted_iota(jnp.int32, (8, B), 0)
    lane = lax.broadcasted_iota(jnp.int32, (8, B), 1)
    halves = WIDE // 8
    steps = B // WIDE
    for g in range(steps):
        mine = [halves * g + h for h in range(halves)]
        ahead = [halves * (g + 1) + h for h in range(halves)] if g + 1 < steps else []
        lo = WIDE * g
        inside = (lane >= lo) & (lane < lo + WIDE)
        cols = [[column_of(block[m], lo + c) for m in mine] for c in range(WIDE)]
        rows = jnp.concatenate([block[m] for m in mine], axis=0)
        right = [
            jnp.where(inside, jnp.where(lane - lo - 8 * h == sub, -1.0, 0.0), block[m])
            for h, m in enumerate(mine)
        ]
        later = {j: [column_of(block[j], lo + c) for c in range(WIDE)] for j in ahead}
        for p in range(WIDE // 2):
            r0, r1 = 2 * p, 2 * p + 1
            h, s0, s1 = r0 // 8, r0 % 8, r0 % 8 + 1
            a, b, c = row_of(cols[r0][h], s0), row_of(cols[r1][h], s0), row_of(cols[r1][h], s1)
            inverse = pl.reciprocal(a * c - b * b)
            at0, at1 = sub == s0, sub == s1
            both = at0 | at1
            n0, n1 = [], []
            for k in range(halves):
                x0 = cols[r0][k] * c - cols[r1][k] * b
                x1 = cols[r1][k] * a - cols[r0][k] * b
                if k == h:
                    x0 = jnp.where(at0, -c, jnp.where(at1, b, x0))
                    x1 = jnp.where(at0, b, jnp.where(at1, -a, x1))
                n0.append(x0)
                n1.append(x1)

            def swept(column):
                u, v = row_of(column[h], s0), row_of(column[h], s1)
                out = []
                for k in range(halves):
                    old = jnp.where(both, 0.0, column[k]) if k == h else column[k]
                    out.append(old - (n0[k] * u + n1[k] * v) * inverse)
                return out

            for q in range(r1 + 1, WIDE):
                cols[q] = swept(cols[q])
            right = swept(right)
        outer = full_dot(rows, jnp.concatenate(right, axis=0), (0, 0))
        terms = [row_of(right[c // 8], c % 8) for c in range(WIDE)] if ahead else None
        for j in range(B // 8):
            if j in mine:
                block[j] = right[j - mine[0]]
            elif j in ahead:
                value = jnp.where(inside, 0.0, block[j])
                for c in range(WIDE):
                    value = value - later[j][c] * terms[c]
                block[j] = value
            else:
                block[j] = jnp.where(inside, 0.0, block[j]) - outer[8 * j : 8 * j + 8, :]
    return jnp.concatenate(block, axis=0)


def solve_in_place(system, ridge):
    f, width = system.shape
    count = f // B
    diagonal = lax.broadcasted_iota(jnp.int32, (B, B), 0) == lax.broadcasted_iota(jnp.int32, (B, B), 1)
    for j in range(count):
        here = pl.ds(j * B, B)
        block = system[here, here] + jnp.where(diagonal, ridge, 0.0)
        inverse = negative_inverse([block[8 * i : 8 * i + 8, :] for i in range(B // 8)])
        rest = system[here, pl.ds((j + 1) * B, width - (j + 1) * B)]
        turned = full_dot(inverse, rest)
        system[here, pl.ds((j + 1) * B, width - (j + 1) * B)] = turned
        for k in range(j + 1, count):
            at = (k - j - 1) * B
            part = pl.ds(k * B, width - k * B)
            system[pl.ds(k * B, B), part] += full_dot(rest[:, at : at + B], turned[:, at:], (0, 0))
    last = pl.ds(f, width - f)
    for j in range(count - 2, -1, -1):
        here = pl.ds(j * B, B)
        behind = pl.ds((j + 1) * B, f - (j + 1) * B)
        system[here, last] += full_dot(system[here, behind], system[behind, last])


def fit_kernel(tile, counts_ref, codes_ref, system_ref, x_hbm, y_hbm, out_ref, error_ref, system, x, y, sems):
    n, f = x.shape
    r = y.shape[1]
    get_x = pltpu.make_async_copy(x_hbm, x, sems.at[0])
    get_y = pltpu.make_async_copy(y_hbm, y, sems.at[1])
    get_x.start()
    get_y.start()
    for j in range(f // B):
        width = f + r - j * B
        system[pl.ds(j * B, B), pl.ds(j * B, width)] = system_ref[:, pl.ds(packed(j, j, f, f + r), width)]
    shard = shard_index()
    seen = jnp.int32(0)
    for k in range(counts_ref.shape[0]):
        seen += jnp.where(k < shard, counts_ref[k], 0)
    first = (shard == 0).astype(F32)
    ridge = codes_ref[jnp.maximum(shard - 1, 0)].astype(F32) * seen.astype(F32) * 0.0625 + first
    solve_in_place(system, ridge)
    weights = -system[:, pl.ds(f, r)] * (1.0 - first)
    valid_rows = valid_here(counts_ref, n)
    wh, wl = halves_of(weights)
    both = jnp.concatenate([wh, wl], axis=1)
    get_x.wait()
    get_y.wait()
    error_ref[...] = jnp.zeros_like(error_ref)

    @pl.loop(0, n // tile)
    def _(i):
        here = pl.ds(pl.multiple_of(i * tile, tile), tile)
        xh, xl = halves_of(x[here, :])
        first = mxu(xh, both)
        value = first[:, :r] + first[:, r:] + mxu(xl, wh)
        valid = i * tile + lax.broadcasted_iota(jnp.int32, (tile, r), 0) < valid_rows
        value = jnp.where(valid, value, 0.0)
        out_ref[here, :] = value.astype(BF)
        gap = jnp.where(valid, y[here, :] - value, 0.0)
        error_ref[...] += jnp.sum((gap * gap).reshape(tile // 8, 8, r), axis=0)


def fit_and_predict(system, features, targets, counts, codes):
    n, f = features.shape
    r = targets.shape[1]
    smem, vmem = pl.BlockSpec(memory_space=pltpu.SMEM), pl.BlockSpec(memory_space=pltpu.VMEM)
    anywhere = pl.BlockSpec(memory_space=pl.ANY)
    return pl.pallas_call(
        functools.partial(fit_kernel, 2048),
        in_specs=[smem, smem, vmem, anywhere, anywhere],
        out_specs=[vmem, vmem],
        out_shape=[jax.ShapeDtypeStruct((n, r), BF), jax.ShapeDtypeStruct((8, r), F32)],
        scratch_shapes=[
            pltpu.VMEM((f, f + r), F32),
            pltpu.VMEM((n, f), F32),
            pltpu.VMEM((n, r), F32),
            pltpu.SemaphoreType.DMA((2,)),
        ],
        compiler_params=pltpu.CompilerParams(vmem_limit_bytes=56 * 2**20),
        name="fit",
    )(counts, codes, system, features, targets)


def split_tile(i, tile, valid_rows, x, y, xh, xl, yh, yl):
    here = pl.ds(pl.multiple_of(i * tile, tile), tile)
    valid = i * tile + lax.broadcasted_iota(jnp.int32, (tile, 1), 0) < valid_rows
    xh[here, :], xl[here, :] = halves_of(jnp.where(valid, x[here, :], 0.0))
    yh[here, :], yl[here, :] = halves_of(y[here, :])


def upper_products(i, tile, xh, xl, yh, yl, upper, mirror, turned):
    here = pl.ds(pl.multiple_of(i * tile, tile), tile)
    half = xh.shape[1] // 2
    left, right = xh[here, :half], xh[here, half:]
    low = xl[here, :]
    high = yh[here, :]
    upper[...] += mxu(left, jnp.concatenate([high, yl[here, :], low, left, right], axis=1), (0, 0))
    mirror[...] += mxu(right, low[:, :half], (0, 0))
    turned[...] += mxu(high, low, (0, 0))


def lower_products(i, tile, xh, xl, yh, yl, lower):
    here = pl.ds(pl.multiple_of(i * tile, tile), tile)
    half = xh.shape[1] // 2
    right = xh[here, half:]
    lower[...] += mxu(right, jnp.concatenate([yh[here, :], yl[here, :], xl[here, half:], right], axis=1), (0, 0))


def pack_upper(out, upper, mirror, turned, f, r):
    half = f // 2
    for i in range(half // B):
        here = pl.ds(i * B, B)
        for j in range(i, f // B):
            b = pl.ds(packed(i, j, f, f + r), B)
            out[:, b] = upper[here, pl.ds(2 * r + f + j * B, B)]
            out[:, b] += upper[here, pl.ds(2 * r + j * B, B)]
            other = upper if j * B < half else mirror
            at = 2 * r if j * B < half else 0
            out[:, b] += other[pl.ds(j * B % half, B), pl.ds(at + i * B, B)].T
        pack_cross(out, i, upper, turned, f, r)


def pack_lower(out, lower, turned, f, r):
    half = f // 2
    for i in range(half // B, f // B):
        here = pl.ds(i * B - half, B)
        for j in range(i, f // B):
            b = pl.ds(packed(i, j, f, f + r), B)
            out[:, b] = lower[here, pl.ds(2 * r + j * B, B)]
            out[:, b] += lower[here, pl.ds(2 * r + j * B - half, B)]
            out[:, b] += lower[pl.ds(j * B - half, B), pl.ds(2 * r + i * B - half, B)].T
        pack_cross(out, i, lower, turned, f, r)


def pack_cross(out, i, acc, turned, f, r):
    here = pl.ds(i * B % (f // 2), B)
    b = pl.ds(packed(i, f // B, f, f + r), r)
    out[:, b] = acc[here, pl.ds(0, r)]
    out[:, b] += acc[here, pl.ds(r, r)]
    out[:, b] += turned[:, pl.ds(i * B, B)].T


def prefix_kernel(
    chunks,
    tile,
    counts_ref,
    x_hbm,
    y_hbm,
    out_ref,
    xf,
    yf,
    xh,
    xl,
    yh,
    yl,
    upper,
    mirror,
    lower,
    turned,
    part_ref,
    twin_in,
    pair,
    row_in,
    mine,
    z_in,
    before,
    through,
    x_in,
    full,
    loads,
    sends,
    arrivals,
):
    z, x, r = lax.axis_index("tm_0"), lax.axis_index("tm_1"), lax.axis_index("rows")
    y, core = r // 2, lax.rem(r, 2)
    twin = {"rows": r + 1 - 2 * core}
    count, half, piece = len(chunks), B // 2, B // 8

    def other(i, d):
        return lax.rem(i + d, 4)

    barrier = pltpu.get_barrier_semaphore()
    pl.semaphore_signal(barrier, inc=1, device_id=twin, device_id_type=MESH)
    for d in (1, 2, 3):
        for peer in ({"rows": 2 * other(y, d) + core}, {"tm_0": other(z, d)}, {"tm_1": other(x, d)}):
            pl.semaphore_signal(barrier, inc=1, device_id=peer, device_id_type=MESH)
    def load(i):
        here = pl.ds(pl.multiple_of(i * tile, tile), tile)
        return (
            pltpu.make_async_copy(x_hbm.at[here], xf.at[here], loads.at[2 * i]),
            pltpu.make_async_copy(y_hbm.at[here], yf.at[here], loads.at[2 * i + 1]),
        )

    n, f = xf.shape
    targets = yf.shape[1]
    tiles = n // tile
    for i in range(tiles):
        for copy in load(i):
            copy.start()
    valid_rows = valid_here(counts_ref, n)
    for acc in (upper, mirror, lower, turned):
        acc[...] = jnp.zeros_like(acc)

    def send(phase, j, d, src, dst, peer):
        at = (phase * count + j) * 3 + d - 1
        return pltpu.make_async_remote_copy(
            src_ref=src,
            dst_ref=dst,
            send_sem=sends.at[at],
            recv_sem=arrivals.at[at],
            device_id=peer,
            device_id_type=MESH,
        )

    def multiple(i):
        return pl.multiple_of(i, piece)

    def part(ref, j, start, size, d=None):
        rows = pl.ds(start if isinstance(start, int) else multiple(start), size)
        where = (rows, pl.ds(*chunks[j]))
        return ref.at[where] if d is None else ref.at[(d - 1, *where)]

    def small(ref, j, d=None):
        return part(ref, j, 0, piece, d)

    def to_twin(j):
        return send(0, j, 1, part(part_ref, j, half * (1 - core), half), part(twin_in, j, 0, half), twin)

    def to_row(j, d):
        to = other(y, d)
        return send(1, j, d, part(pair, j, piece * to, piece), small(row_in, j, d), {"rows": 2 * to + core})

    def to_z(j, d):
        return send(2, j, d, small(mine, j), small(z_in, j, d), {"tm_0": other(z, d)})

    def to_x(j, d, src):
        return send(3, j, d, small(src, j), small(x_in, j, d), {"tm_1": other(x, d)})

    def own(j):
        return part(full, j, half * core + piece * y, piece)

    def spread_row(j, d):
        return send(4, j, d, own(j), own(j), {"rows": 2 * other(y, d) + core})

    def row_arrival(j, d):
        there = part(full, j, half * core + piece * other(y, 4 - d), piece)
        return send(4, j, d, there, there, twin)

    def spread_twin(j):
        ours = part(full, j, half * core, half)
        return send(5, j, 1, ours, ours, twin)

    def twin_arrival(j):
        there = part(full, j, half * (1 - core), half)
        return send(5, j, 1, there, there, twin)

    def stage(p, j):
        if p == 0:
            to_twin(j).start()
        if p == 1:
            to_twin(j).wait_recv()
            part(pair, j, 0, half)[...] = (
                part(part_ref, j, half * core, half)[...] + part(twin_in, j, 0, half)[...]
            )
            for d in (1, 2, 3):
                to_row(j, d).start()
        if p == 2:
            total = part(pair, j, piece * y, piece)[...]
            for d in (1, 2, 3):
                to_row(j, d).wait_recv()
                total += small(row_in, j, d)[...]
            small(mine, j)[...] = total
            small(before, j)[...] = jnp.zeros_like(total)
            for d in (1, 2, 3):
                pl.when(z + d < 4)(lambda d=d: to_z(j, d).start())
        if p == 3:
            for d in (1, 2, 3):

                @pl.when(z >= d)
                def _(d=d):
                    to_z(j, d).wait_recv()
                    small(before, j)[...] += small(z_in, j, d)[...]

            small(through, j)[...] = small(before, j)[...] + small(mine, j)[...]
            for d in (1, 2, 3):
                pl.when(x + d < 4)(lambda d=d: to_x(j, d, through).start())
                pl.when(x + d >= 4)(lambda d=d: to_x(j, d, before).start())
        if p == 4:
            total = small(before, j)[...]
            for d in (1, 2, 3):
                to_x(j, d, before).wait_recv()
                total += small(x_in, j, d)[...]
            own(j)[...] = total
            for d in (1, 2, 3):
                spread_row(j, d).start()
        if p == 5:
            for d in (1, 2, 3):
                row_arrival(j, d).wait_recv()
            spread_twin(j).start()
        if p == 6:
            twin_arrival(j).wait_recv()
            part(out_ref, j, 0, B)[...] = part(full, j, 0, B)[...]

    def split(i):
        for copy in load(i):
            copy.wait()
        split_tile(i, tile, valid_rows, xf, yf, xh, xl, yh, yl)

    split(0)

    @pl.loop(1, tiles)
    def _(i):
        upper_products(i - 1, tile, xh, xl, yh, yl, upper, mirror, turned)
        split(i)

    upper_products(tiles - 1, tile, xh, xl, yh, yl, upper, mirror, turned)
    pack_upper(part_ref, upper, mirror, turned, f, targets)
    pl.semaphore_wait(barrier, 10)
    stage(0, 0)
    early = 2

    @pl.loop(0, early)
    def _(i):
        lower_products(i, tile, xh, xl, yh, yl, lower)

    stage(1, 0)

    @pl.loop(early, tiles)
    def _(i):
        lower_products(i, tile, xh, xl, yh, yl, lower)

    pack_lower(part_ref, lower, turned, f, targets)
    stage(0, 1)
    for p in range(2, 7):
        stage(p, 0)
        stage(p - 1, 1)
    stage(6, 1)
    for j in range(count):
        to_twin(j).wait_send()
        spread_twin(j).wait_send()
        for d in (1, 2, 3):
            to_row(j, d).wait_send()
            pl.when(z + d < 4)(lambda d=d: to_z(j, d).wait_send())
            to_x(j, d, before).wait_send()
            spread_row(j, d).wait_send()


def prefix_of_shards(features, targets, counts):
    n, f = features.shape
    r = targets.shape[1]
    half, tile = f // 2, 1024
    first, columns = packed(half // B, half // B, f, f + r), packed(f // B, f // B, f, f + r)
    chunks = [(0, first), (first, columns - first)]
    pair, piece = (B // 2, columns), (B // 8, columns)
    anywhere = pl.BlockSpec(memory_space=pl.ANY)
    return pl.pallas_call(
        functools.partial(prefix_kernel, chunks, tile),
        in_specs=[pl.BlockSpec(memory_space=pltpu.SMEM), anywhere, anywhere],
        out_specs=pl.BlockSpec(memory_space=pltpu.VMEM),
        out_shape=jax.ShapeDtypeStruct((B, columns), F32),
        scratch_shapes=[
            pltpu.VMEM((n, f), F32),
            pltpu.VMEM((n, r), F32),
            pltpu.VMEM((n, f), BF),
            pltpu.VMEM((n, f), BF),
            pltpu.VMEM((n, r), BF),
            pltpu.VMEM((n, r), BF),
            pltpu.VMEM((half, 2 * f + 2 * r), F32),
            pltpu.VMEM((half, half), F32),
            pltpu.VMEM((half, f + 2 * r), F32),
            pltpu.VMEM((r, f), F32),
            pltpu.VMEM((B, columns), F32),
            pltpu.VMEM(pair, F32),
            pltpu.VMEM(pair, F32),
            pltpu.VMEM((3, *piece), F32),
            pltpu.VMEM(piece, F32),
            pltpu.VMEM((3, *piece), F32),
            pltpu.VMEM(piece, F32),
            pltpu.VMEM(piece, F32),
            pltpu.VMEM((3, *piece), F32),
            pltpu.VMEM((B, columns), F32),
            pltpu.SemaphoreType.DMA((2 * n // tile,)),
            pltpu.SemaphoreType.DMA((18 * len(chunks),)),
            pltpu.SemaphoreType.DMA((18 * len(chunks),)),
        ],
        compiler_params=pltpu.CompilerParams(
            collective_id=0, has_side_effects=True, vmem_limit_bytes=58 * 2**20
        ),
        name="prefix",
    )(counts, features, targets)


def error_kernel(targets, counts_ref, error_ref, out_ref, gathered, sends, arrivals):
    r = lax.axis_index("rows")
    size = lax.axis_size("rows")

    def peer(d):
        return {"rows": lax.rem(r + d, size)}

    barrier = pltpu.get_barrier_semaphore()
    for d in range(1, size):
        pl.semaphore_signal(barrier, inc=1, device_id=peer(d), device_id_type=MESH)
    pl.semaphore_wait(barrier, size - 1)
    copies = [
        pltpu.make_async_remote_copy(
            src_ref=error_ref,
            dst_ref=gathered.at[d - 1],
            send_sem=sends.at[d - 1],
            recv_sem=arrivals.at[d - 1],
            device_id=peer(d),
            device_id_type=MESH,
        )
        for d in range(1, size)
    ]
    for copy in copies:
        copy.start()
    total = error_ref[...]
    for d, copy in enumerate(copies):
        copy.wait_recv()
        total += gathered[d]
    out_ref[0] = jnp.sum(total) / (counts_ref[shard_index()].astype(F32) * targets)
    for copy in copies:
        copy.wait_send()


def mean_error(errors, counts, targets):
    size = lax.axis_size("rows")
    smem, vmem = pl.BlockSpec(memory_space=pltpu.SMEM), pl.BlockSpec(memory_space=pltpu.VMEM)
    return pl.pallas_call(
        functools.partial(error_kernel, targets),
        in_specs=[smem, vmem],
        out_specs=smem,
        out_shape=jax.ShapeDtypeStruct((1,), F32),
        scratch_shapes=[
            pltpu.VMEM((size - 1, *errors.shape), F32),
            pltpu.SemaphoreType.DMA((size - 1,)),
            pltpu.SemaphoreType.DMA((size - 1,)),
        ],
        compiler_params=pltpu.CompilerParams(collective_id=1, has_side_effects=True),
        name="error",
    )(counts, errors)


def body(features, targets, row_counts, ridge_codes):
    system = prefix_of_shards(features, targets, row_counts)
    forecast, errors = fit_and_predict(system, features, targets, row_counts, ridge_codes)
    return forecast, mean_error(errors, row_counts, targets.shape[1])


def solution(mesh):
    finer = Mesh(mesh.devices.reshape(4, 4, mesh.shape["rows"]), ("tm_0", "tm_1", "rows"))
    placed = (P(TM_ROWS, None), P(TM_ROWS, None), P(), P())
    return jax.shard_map(
        body, mesh=finer, in_specs=placed, out_specs=(P(TM_ROWS, None), P(TM)), check_vma=False
    )
```

```python
import functools

import jax
import jax.numpy as jnp
from jax import lax
from jax.experimental import pallas as pl
from jax.experimental.pallas import tpu as pltpu
from jax.sharding import Mesh
from jax.sharding import PartitionSpec as P

TM = ("tm_0", "tm_1")
TM_ROWS = ("tm_0", "tm_1", "rows")
F32 = jnp.float32
BF = jnp.bfloat16
B = 128
WIDE = 16
MESH = pl.DeviceIdType.MESH


def halves_of(x):
    high = x.astype(BF)
    return high, (x - high.astype(F32)).astype(BF)


def thirds_of(x):
    high = x.astype(BF)
    left = x - high.astype(F32)
    middle = left.astype(BF)
    return high, middle, (left - middle.astype(F32)).astype(BF)


def mxu(left, right, dims=(1, 0)):
    contract = (((dims[0],), (dims[1],)), ((), ()))
    return lax.dot_general(left, right, contract, preferred_element_type=F32)


def packed(i, j, f, width):
    return sum(width - k * B for k in range(i)) + (j - i) * B


def full_dot(a, b, dims=(1, 0)):
    ah, am, al = thirds_of(a)
    bh, bm, bl = thirds_of(b)
    left = jnp.concatenate([ah, ah, am, am, ah, al], axis=dims[0])
    right = jnp.concatenate([bh, bm, bh, bm, bl, bh], axis=dims[1])
    return mxu(left, right, dims)


def shard_index():
    return lax.axis_index("tm_0") * lax.axis_size("tm_1") + lax.axis_index("tm_1")


def valid_here(counts_ref, rows):
    return counts_ref[shard_index()] - lax.axis_index("rows") * rows


def row_of(x, s):
    return jnp.take_along_axis(x, jnp.full((8, B), s, jnp.int32), axis=0)


def column_of(x, c):
    return jnp.broadcast_to(x[:, c : c + 1], (8, B))


def negative_inverse(block):
    block = list(block)
    sub = lax.broadcasted_iota(jnp.int32, (8, B), 0)
    lane = lax.broadcasted_iota(jnp.int32, (8, B), 1)
    halves = WIDE // 8
    steps = B // WIDE
    for g in range(steps):
        mine = [halves * g + h for h in range(halves)]
        ahead = [halves * (g + 1) + h for h in range(halves)] if g + 1 < steps else []
        lo = WIDE * g
        inside = (lane >= lo) & (lane < lo + WIDE)
        cols = [[column_of(block[m], lo + c) for m in mine] for c in range(WIDE)]
        rows = jnp.concatenate([block[m] for m in mine], axis=0)
        right = [
            jnp.where(inside, jnp.where(lane - lo - 8 * h == sub, -1.0, 0.0), block[m])
            for h, m in enumerate(mine)
        ]
        later = {j: [column_of(block[j], lo + c) for c in range(WIDE)] for j in ahead}
        for p in range(WIDE // 2):
            r0, r1 = 2 * p, 2 * p + 1
            h, s0, s1 = r0 // 8, r0 % 8, r0 % 8 + 1
            a, b, c = row_of(cols[r0][h], s0), row_of(cols[r1][h], s0), row_of(cols[r1][h], s1)
            inverse = pl.reciprocal(a * c - b * b)
            at0, at1 = sub == s0, sub == s1
            both = at0 | at1
            n0, n1 = [], []
            for k in range(halves):
                x0 = cols[r0][k] * c - cols[r1][k] * b
                x1 = cols[r1][k] * a - cols[r0][k] * b
                if k == h:
                    x0 = jnp.where(at0, -c, jnp.where(at1, b, x0))
                    x1 = jnp.where(at0, b, jnp.where(at1, -a, x1))
                n0.append(x0)
                n1.append(x1)

            def swept(column):
                u, v = row_of(column[h], s0), row_of(column[h], s1)
                out = []
                for k in range(halves):
                    old = jnp.where(both, 0.0, column[k]) if k == h else column[k]
                    out.append(old - (n0[k] * u + n1[k] * v) * inverse)
                return out

            for q in range(r1 + 1, WIDE):
                cols[q] = swept(cols[q])
            right = swept(right)
        outer = full_dot(rows, jnp.concatenate(right, axis=0), (0, 0))
        terms = [row_of(right[c // 8], c % 8) for c in range(WIDE)] if ahead else None
        for j in range(B // 8):
            if j in mine:
                block[j] = right[j - mine[0]]
            elif j in ahead:
                value = jnp.where(inside, 0.0, block[j])
                for c in range(WIDE):
                    value = value - later[j][c] * terms[c]
                block[j] = value
            else:
                block[j] = jnp.where(inside, 0.0, block[j]) - outer[8 * j : 8 * j + 8, :]
    return jnp.concatenate(block, axis=0)


def solve(rows_of, system, scaled, ridge):
    f, width = system.shape
    count = f // B
    diagonal = lax.broadcasted_iota(jnp.int32, (B, B), 0) == lax.broadcasted_iota(jnp.int32, (B, B), 1)
    for k in range(count):
        here, part = pl.ds(k * B, B), pl.ds(k * B, width - k * B)
        system[here, part] = rows_of(k)
        if k:
            earlier = pl.ds(0, k * B)
            system[here, part] += full_dot(system[earlier, here], scaled[earlier, part], (0, 0))
        block = system[here, here] + jnp.where(diagonal, ridge, 0.0)
        inverse = negative_inverse([block[8 * i : 8 * i + 8, :] for i in range(B // 8)])
        rest = pl.ds((k + 1) * B, width - (k + 1) * B)
        scaled[here, rest] = full_dot(inverse, system[here, rest])
    last = pl.ds(f, width - f)
    for j in range(count - 2, -1, -1):
        here, behind = pl.ds(j * B, B), pl.ds((j + 1) * B, f - (j + 1) * B)
        scaled[here, last] += full_dot(scaled[here, behind], scaled[behind, last])


def predict(tile, solution_part, scale, valid_rows, xh, xl, y, out_ref, error):
    n, r = y.shape
    wh, wl = halves_of(solution_part * scale)
    both = jnp.concatenate([wh, wl], axis=1)
    error[...] = jnp.zeros_like(error)

    @pl.loop(0, n // tile)
    def _(i):
        here = pl.ds(pl.multiple_of(i * tile, tile), tile)
        first = mxu(xh[here, :], both)
        value = first[:, :r] + first[:, r:] + mxu(xl[here, :], wh)
        out_ref[here, :] = value.astype(BF)
        valid = i * tile + lax.broadcasted_iota(jnp.int32, (tile, r), 0) < valid_rows
        gap = jnp.where(valid, y[here, :] - value, 0.0)
        error[...] += jnp.sum((gap * gap).reshape(tile // 8, 8, r), axis=0)


def split_tile(i, tile, valid_rows, x, y, xh, xl, yh, yl):
    here = pl.ds(pl.multiple_of(i * tile, tile), tile)
    valid = i * tile + lax.broadcasted_iota(jnp.int32, (tile, 1), 0) < valid_rows
    xh[here, :], xl[here, :] = halves_of(jnp.where(valid, x[...], 0.0))
    yh[here, :], yl[here, :] = halves_of(y[here, :])


def upper_products(i, tile, xh, xl, yh, yl, upper, mirror, turned):
    here = pl.ds(pl.multiple_of(i * tile, tile), tile)
    half = xh.shape[1] // 2
    left, right = xh[here, :half], xh[here, half:]
    low = xl[here, :]
    high = yh[here, :]
    upper[...] += mxu(left, jnp.concatenate([high, yl[here, :], low, left, right], axis=1), (0, 0))
    mirror[...] += mxu(right, low[:, :half], (0, 0))
    turned[...] += mxu(high, low, (0, 0))


def lower_products(i, tile, xh, xl, yh, yl, lower):
    here = pl.ds(pl.multiple_of(i * tile, tile), tile)
    half = xh.shape[1] // 2
    right = xh[here, half:]
    lower[...] += mxu(right, jnp.concatenate([yh[here, :], yl[here, :], xl[here, half:], right], axis=1), (0, 0))


def pack_upper(out, upper, mirror, turned, f, r):
    half = f // 2
    for i in range(half // B):
        here = pl.ds(i * B, B)
        for j in range(i, f // B):
            b = pl.ds(packed(i, j, f, f + r), B)
            out[:, b] = upper[here, pl.ds(2 * r + f + j * B, B)]
            out[:, b] += upper[here, pl.ds(2 * r + j * B, B)]
            other = upper if j * B < half else mirror
            at = 2 * r if j * B < half else 0
            out[:, b] += other[pl.ds(j * B % half, B), pl.ds(at + i * B, B)].T
        pack_cross(out, i, upper, turned, f, r)


def pack_lower(out, lower, turned, f, r):
    half = f // 2
    for i in range(half // B, f // B):
        here = pl.ds(i * B - half, B)
        for j in range(i, f // B):
            b = pl.ds(packed(i, j, f, f + r), B)
            out[:, b] = lower[here, pl.ds(2 * r + j * B, B)]
            out[:, b] += lower[here, pl.ds(2 * r + j * B - half, B)]
            out[:, b] += lower[pl.ds(j * B - half, B), pl.ds(2 * r + i * B - half, B)].T
        pack_cross(out, i, lower, turned, f, r)


def pack_cross(out, i, acc, turned, f, r):
    here = pl.ds(i * B % (f // 2), B)
    b = pl.ds(packed(i, f // B, f, f + r), r)
    out[:, b] = acc[here, pl.ds(0, r)]
    out[:, b] += acc[here, pl.ds(r, r)]
    out[:, b] += turned[:, pl.ds(i * B, B)].T


def backtest_kernel(
    chunks,
    tile,
    counts_ref,
    codes_ref,
    x_hbm,
    y_hbm,
    out_ref,
    mse_ref,
    xf,
    yf,
    xh,
    xl,
    yh,
    yl,
    upper,
    mirror,
    lower,
    turned,
    part_ref,
    twin_in,
    pair,
    row_in,
    mine,
    z_in,
    before,
    through,
    x_in,
    full,
    system,
    scaled,
    error,
    errors_in,
    loads,
    sends,
    arrivals,
    error_sends,
    error_arrivals,
):
    z, x, r = lax.axis_index("tm_0"), lax.axis_index("tm_1"), lax.axis_index("rows")
    y, core = r // 2, lax.rem(r, 2)
    twin = {"rows": r + 1 - 2 * core}
    count, half, piece = len(chunks), B // 2, B // 8

    def other(i, d):
        return lax.rem(i + d, 4)

    barrier = pltpu.get_barrier_semaphore()
    size = lax.axis_size("rows")
    neighbours = [{"rows": lax.rem(r + d, size)} for d in range(1, size)]
    for d in (1, 2, 3):
        neighbours += [{"tm_0": other(z, d)}, {"tm_1": other(x, d)}]
    for peer in neighbours:
        pl.semaphore_signal(barrier, inc=1, device_id=peer, device_id_type=MESH)
    def load(i):
        here = pl.ds(pl.multiple_of(i * tile, tile), tile)
        return (
            pltpu.make_async_copy(x_hbm.at[here], xf.at[lax.rem(i, slots)], loads.at[2 * i]),
            pltpu.make_async_copy(y_hbm.at[here], yf.at[here], loads.at[2 * i + 1]),
        )

    n, f = xh.shape
    slots = xf.shape[0]
    targets = yf.shape[1]
    tiles = n // tile
    for i in range(slots):
        for copy in load(i):
            copy.start()
    valid_rows = valid_here(counts_ref, n)
    for acc in (upper, mirror, lower, turned):
        acc[...] = jnp.zeros_like(acc)

    def send(phase, j, d, src, dst, peer):
        at = (phase * count + j) * 3 + d - 1
        return pltpu.make_async_remote_copy(
            src_ref=src,
            dst_ref=dst,
            send_sem=sends.at[at],
            recv_sem=arrivals.at[at],
            device_id=peer,
            device_id_type=MESH,
        )

    def multiple(i):
        return pl.multiple_of(i, piece)

    def part(ref, j, start, size, d=None):
        rows = pl.ds(start if isinstance(start, int) else multiple(start), size)
        where = (rows, pl.ds(*chunks[j]))
        return ref.at[where] if d is None else ref.at[(d - 1, *where)]

    def small(ref, j, d=None):
        return part(ref, j, 0, piece, d)

    def to_twin(j):
        return send(0, j, 1, part(part_ref, j, half * (1 - core), half), part(twin_in, j, 0, half), twin)

    def to_row(j, d):
        to = other(y, d)
        return send(1, j, d, part(pair, j, piece * to, piece), small(row_in, j, d), {"rows": 2 * to + core})

    def to_z(j, d):
        return send(2, j, d, small(mine, j), small(z_in, j, d), {"tm_0": other(z, d)})

    def to_x(j, d, src):
        return send(3, j, d, small(src, j), small(x_in, j, d), {"tm_1": other(x, d)})

    def own(j):
        return part(full, j, half * core + piece * y, piece)

    def spread_row(j, d):
        return send(4, j, d, own(j), own(j), {"rows": 2 * other(y, d) + core})

    def row_arrival(j, d):
        there = part(full, j, half * core + piece * other(y, 4 - d), piece)
        return send(4, j, d, there, there, twin)

    def spread_twin(j):
        ours = part(full, j, half * core, half)
        return send(5, j, 1, ours, ours, twin)

    def twin_arrival(j):
        there = part(full, j, half * (1 - core), half)
        return send(5, j, 1, there, there, twin)

    def stage(p, j):
        if p == 0:
            to_twin(j).start()
        if p == 1:
            to_twin(j).wait_recv()
            part(pair, j, 0, half)[...] = (
                part(part_ref, j, half * core, half)[...] + part(twin_in, j, 0, half)[...]
            )
            for d in (1, 2, 3):
                to_row(j, d).start()
        if p == 2:
            total = part(pair, j, piece * y, piece)[...]
            for d in (1, 2, 3):
                to_row(j, d).wait_recv()
                total += small(row_in, j, d)[...]
            small(mine, j)[...] = total
            small(before, j)[...] = jnp.zeros_like(total)
            for d in (1, 2, 3):
                pl.when(z + d < 4)(lambda d=d: to_z(j, d).start())
        if p == 3:
            for d in (1, 2, 3):

                @pl.when(z >= d)
                def _(d=d):
                    to_z(j, d).wait_recv()
                    small(before, j)[...] += small(z_in, j, d)[...]

            small(through, j)[...] = small(before, j)[...] + small(mine, j)[...]
            for d in (1, 2, 3):
                pl.when(x + d < 4)(lambda d=d: to_x(j, d, through).start())
                pl.when(x + d >= 4)(lambda d=d: to_x(j, d, before).start())
        if p == 4:
            total = small(before, j)[...]
            for d in (1, 2, 3):
                to_x(j, d, before).wait_recv()
                total += small(x_in, j, d)[...]
            own(j)[...] = total
            for d in (1, 2, 3):
                spread_row(j, d).start()
        if p == 5:
            for d in (1, 2, 3):
                row_arrival(j, d).wait_recv()
            spread_twin(j).start()
        if p == 6:
            twin_arrival(j).wait_recv()

    def split(i):
        for copy in load(i):
            copy.wait()
        split_tile(i, tile, valid_rows, xf.at[lax.rem(i, slots)], yf, xh, xl, yh, yl)

    split(0)

    @pl.loop(1, tiles)
    def _(i):
        @pl.when(i + slots - 1 < tiles)
        def _():
            for copy in load(i + slots - 1):
                copy.start()

        upper_products(i - 1, tile, xh, xl, yh, yl, upper, mirror, turned)
        split(i)

    upper_products(tiles - 1, tile, xh, xl, yh, yl, upper, mirror, turned)
    pack_upper(part_ref, upper, mirror, turned, f, targets)
    pl.semaphore_wait(barrier, len(neighbours))
    stage(0, 0)
    early = 2

    @pl.loop(0, early)
    def _(i):
        lower_products(i, tile, xh, xl, yh, yl, lower)

    stage(1, 0)

    @pl.loop(early, tiles)
    def _(i):
        lower_products(i, tile, xh, xl, yh, yl, lower)

    pack_lower(part_ref, lower, turned, f, targets)
    stage(0, 1)
    for p in range(2, 6):
        stage(p, 0)
        stage(p - 1, 1)
    stage(6, 0)

    shard = shard_index()
    seen = jnp.int32(0)
    for k in range(counts_ref.shape[0]):
        seen += jnp.where(k < shard, counts_ref[k], 0)
    first = (shard == 0).astype(F32)
    ridge = codes_ref[jnp.maximum(shard - 1, 0)].astype(F32) * seen.astype(F32) * 0.0625 + first
    columns = f + targets

    def rows_of(k):
        if k == 1:
            stage(5, 1)
        if 2 * k * B == f:
            stage(6, 1)
        return full[:, pl.ds(packed(k, k, f, columns), columns - k * B)]

    solve(rows_of, system, scaled, ridge)
    predict(2 * tile, scaled[:, pl.ds(f, targets)], first - 1.0, valid_rows, xh, xl, yf, out_ref, error)

    errors_in[r] = error[...]

    def send_error(d, slot):
        return pltpu.make_async_remote_copy(
            src_ref=error,
            dst_ref=errors_in.at[slot],
            send_sem=error_sends.at[d - 1],
            recv_sem=error_arrivals.at[d - 1],
            device_id=neighbours[d - 1],
            device_id_type=MESH,
        )

    for d in range(1, size):
        send_error(d, r).start()
    for d in range(1, size):
        send_error(d, lax.rem(r + size - d, size)).wait_recv()
    total = errors_in[0]
    for k in range(1, size):
        total += errors_in[k]
    mse_ref[0] = jnp.sum(total) / (counts_ref[shard].astype(F32) * targets)
    for d in range(1, size):
        send_error(d, r).wait_send()
    for j in range(count):
        to_twin(j).wait_send()
        spread_twin(j).wait_send()
        for d in (1, 2, 3):
            to_row(j, d).wait_send()
            pl.when(z + d < 4)(lambda d=d: to_z(j, d).wait_send())
            to_x(j, d, before).wait_send()
            spread_row(j, d).wait_send()


def backtest(features, targets, counts, codes):
    n, f = features.shape
    r = targets.shape[1]
    half, tile = f // 2, 1024
    first, columns = packed(half // B, half // B, f, f + r), packed(f // B, f // B, f, f + r)
    chunks = [(0, first), (first, columns - first)]
    pair, piece = (B // 2, columns), (B // 8, columns)
    size = lax.axis_size("rows")
    smem, anywhere = pl.BlockSpec(memory_space=pltpu.SMEM), pl.BlockSpec(memory_space=pl.ANY)
    return pl.pallas_call(
        functools.partial(backtest_kernel, chunks, tile),
        in_specs=[smem, smem, anywhere, anywhere],
        out_specs=[pl.BlockSpec(memory_space=pltpu.VMEM), smem],
        out_shape=[jax.ShapeDtypeStruct((n, r), BF), jax.ShapeDtypeStruct((1,), F32)],
        scratch_shapes=[
            pltpu.VMEM((4, tile, f), F32),
            pltpu.VMEM((n, r), F32),
            pltpu.VMEM((n, f), BF),
            pltpu.VMEM((n, f), BF),
            pltpu.VMEM((n, r), BF),
            pltpu.VMEM((n, r), BF),
            pltpu.VMEM((half, 2 * f + 2 * r), F32),
            pltpu.VMEM((half, half), F32),
            pltpu.VMEM((half, f + 2 * r), F32),
            pltpu.VMEM((r, f), F32),
            pltpu.VMEM((B, columns), F32),
            pltpu.VMEM(pair, F32),
            pltpu.VMEM(pair, F32),
            pltpu.VMEM((3, *piece), F32),
            pltpu.VMEM(piece, F32),
            pltpu.VMEM((3, *piece), F32),
            pltpu.VMEM(piece, F32),
            pltpu.VMEM(piece, F32),
            pltpu.VMEM((3, *piece), F32),
            pltpu.VMEM((B, columns), F32),
            pltpu.VMEM((f, f + r), F32),
            pltpu.VMEM((f, f + r), F32),
            pltpu.VMEM((8, r), F32),
            pltpu.VMEM((size, 8, r), F32),
            pltpu.SemaphoreType.DMA((2 * n // tile,)),
            pltpu.SemaphoreType.DMA((18 * len(chunks),)),
            pltpu.SemaphoreType.DMA((18 * len(chunks),)),
            pltpu.SemaphoreType.DMA((size - 1,)),
            pltpu.SemaphoreType.DMA((size - 1,)),
        ],
        compiler_params=pltpu.CompilerParams(
            collective_id=0, has_side_effects=True, vmem_limit_bytes=51 * 2**20
        ),
        name="backtest",
    )(counts, codes, features, targets)


def body(features, targets, row_counts, ridge_codes):
    return tuple(backtest(features, targets, row_counts, ridge_codes))


def solution(mesh):
    finer = Mesh(mesh.devices.reshape(4, 4, mesh.shape["rows"]), ("tm_0", "tm_1", "rows"))
    placed = (P(TM_ROWS, None), P(TM_ROWS, None), P(), P())
    return jax.shard_map(
        body, mesh=finer, in_specs=placed, out_specs=(P(TM_ROWS, None), P(TM)), check_vma=False
    )
```

```python
import functools

import jax
import jax.numpy as jnp
from jax import lax
from jax.experimental import pallas as pl
from jax.experimental.pallas import tpu as pltpu
from jax.sharding import Mesh
from jax.sharding import PartitionSpec as P

TM = ("tm_0", "tm_1")
TM_ROWS = ("tm_0", "tm_1", "rows")
F32 = jnp.float32
BF = jnp.bfloat16
B = 128
WIDE = 16
MESH = pl.DeviceIdType.MESH


def halves_of(x):
    high = x.astype(BF)
    return high, (x - high.astype(F32)).astype(BF)


def thirds_of(x):
    high = x.astype(BF)
    left = x - high.astype(F32)
    middle = left.astype(BF)
    return high, middle, (left - middle.astype(F32)).astype(BF)


def mxu(left, right, dims=(1, 0)):
    contract = (((dims[0],), (dims[1],)), ((), ()))
    return lax.dot_general(left, right, contract, preferred_element_type=F32)


def packed(i, j, f, width):
    return sum(width - k * B for k in range(i)) + (j - i) * B


def full_dot(a, b, dims=(1, 0)):
    ah, am, al = thirds_of(a)
    bh, bm, bl = thirds_of(b)
    left = jnp.concatenate([ah, ah, am, am, ah, al], axis=dims[0])
    right = jnp.concatenate([bh, bm, bh, bm, bl, bh], axis=dims[1])
    return mxu(left, right, dims)


def shard_index():
    return lax.axis_index("tm_0") * lax.axis_size("tm_1") + lax.axis_index("tm_1")


def valid_here(counts_ref, rows):
    return counts_ref[shard_index()] - lax.axis_index("rows") * rows


def row_of(x, s):
    return jnp.take_along_axis(x, jnp.full((8, B), s, jnp.int32), axis=0)


def column_of(x, c):
    return jnp.broadcast_to(x[:, c : c + 1], (8, B))


def negative_inverse(block):
    block = list(block)
    sub = lax.broadcasted_iota(jnp.int32, (8, B), 0)
    lane = lax.broadcasted_iota(jnp.int32, (8, B), 1)
    halves = WIDE // 8
    steps = B // WIDE
    for g in range(steps):
        mine = [halves * g + h for h in range(halves)]
        ahead = [halves * (g + 1) + h for h in range(halves)] if g + 1 < steps else []
        lo = WIDE * g
        inside = (lane >= lo) & (lane < lo + WIDE)
        cols = [[column_of(block[m], lo + c) for m in mine] for c in range(WIDE)]
        rows = jnp.concatenate([block[m] for m in mine], axis=0)
        right = [
            jnp.where(inside, jnp.where(lane - lo - 8 * h == sub, -1.0, 0.0), block[m])
            for h, m in enumerate(mine)
        ]
        later = {j: [column_of(block[j], lo + c) for c in range(WIDE)] for j in ahead}
        for p in range(WIDE // 2):
            r0, r1 = 2 * p, 2 * p + 1
            h, s0, s1 = r0 // 8, r0 % 8, r0 % 8 + 1
            a, b, c = row_of(cols[r0][h], s0), row_of(cols[r1][h], s0), row_of(cols[r1][h], s1)
            inverse = pl.reciprocal(a * c - b * b)
            at0, at1 = sub == s0, sub == s1
            both = at0 | at1
            n0, n1 = [], []
            for k in range(halves):
                x0 = cols[r0][k] * c - cols[r1][k] * b
                x1 = cols[r1][k] * a - cols[r0][k] * b
                if k == h:
                    x0 = jnp.where(at0, -c, jnp.where(at1, b, x0))
                    x1 = jnp.where(at0, b, jnp.where(at1, -a, x1))
                n0.append(x0)
                n1.append(x1)

            def swept(column):
                u, v = row_of(column[h], s0), row_of(column[h], s1)
                out = []
                for k in range(halves):
                    old = jnp.where(both, 0.0, column[k]) if k == h else column[k]
                    out.append(old - (n0[k] * u + n1[k] * v) * inverse)
                return out

            for q in range(r1 + 1, WIDE):
                cols[q] = swept(cols[q])
            right = swept(right)
        outer = full_dot(rows, jnp.concatenate(right, axis=0), (0, 0))
        terms = [row_of(right[c // 8], c % 8) for c in range(WIDE)] if ahead else None
        for j in range(B // 8):
            if j in mine:
                block[j] = right[j - mine[0]]
            elif j in ahead:
                value = jnp.where(inside, 0.0, block[j])
                for c in range(WIDE):
                    value = value - later[j][c] * terms[c]
                block[j] = value
            else:
                block[j] = jnp.where(inside, 0.0, block[j]) - outer[8 * j : 8 * j + 8, :]
    return jnp.concatenate(block, axis=0)


def solve(rows_of, system, scaled, ridge):
    f, width = system.shape
    count = f // B
    diagonal = lax.broadcasted_iota(jnp.int32, (B, B), 0) == lax.broadcasted_iota(jnp.int32, (B, B), 1)
    for k in range(count):
        here, part = pl.ds(k * B, B), pl.ds(k * B, width - k * B)
        system[here, part] = rows_of(k)
        if k:
            earlier = pl.ds(0, k * B)
            system[here, part] += full_dot(system[earlier, here], scaled[earlier, part], (0, 0))
        block = system[here, here] + jnp.where(diagonal, ridge, 0.0)
        inverse = negative_inverse([block[8 * i : 8 * i + 8, :] for i in range(B // 8)])
        rest = pl.ds((k + 1) * B, width - (k + 1) * B)
        scaled[here, rest] = full_dot(inverse, system[here, rest])
    last = pl.ds(f, width - f)
    for j in range(count - 2, -1, -1):
        here, behind = pl.ds(j * B, B), pl.ds((j + 1) * B, f - (j + 1) * B)
        scaled[here, last] += full_dot(scaled[here, behind], scaled[behind, last])


def predict(tile, solution_part, scale, valid_rows, xh, xl, y, out_ref, error):
    n, r = y.shape
    wh, wl = halves_of(solution_part * scale)
    both = jnp.concatenate([wh, wl], axis=1)
    error[...] = jnp.zeros_like(error)

    @pl.loop(0, n // tile)
    def _(i):
        here = pl.ds(start_of(i, tile), tile)
        first = mxu(xh[here, :], both)
        value = first[:, :r] + first[:, r:] + mxu(xl[here, :], wh)
        out_ref[here, :] = value.astype(BF)
        valid = i * tile + lax.broadcasted_iota(jnp.int32, (tile, r), 0) < valid_rows
        gap = jnp.where(valid, y[here, :] - value, 0.0)
        error[...] += jnp.sum((gap * gap).reshape(tile // 8, 8, r), axis=0)


def start_of(i, tile):
    return i * tile if isinstance(i, int) else pl.multiple_of(i * tile, tile)


def split_tile(i, tile, valid_rows, x, y, xh, xl, yh, yl):
    here = pl.ds(start_of(i, tile), tile)
    valid = i * tile + lax.broadcasted_iota(jnp.int32, (tile, 1), 0) < valid_rows
    xh[here, :], xl[here, :] = halves_of(jnp.where(valid, x[...], 0.0))
    yh[here, :], yl[here, :] = halves_of(y[here, :])


def upper_products(i, tile, xh, xl, yh, yl, upper, mirror, turned):
    here = pl.ds(start_of(i, tile), tile)
    half = xh.shape[1] // 2
    left, right = xh[here, :half], xh[here, half:]
    low = xl[here, :]
    high = yh[here, :]
    upper[...] += mxu(left, jnp.concatenate([high, yl[here, :], low, left, right], axis=1), (0, 0))
    mirror[...] += mxu(right, low[:, :half], (0, 0))
    turned[...] += mxu(high, low, (0, 0))


def lower_products(i, tile, xh, xl, yh, yl, lower):
    here = pl.ds(start_of(i, tile), tile)
    half = xh.shape[1] // 2
    right = xh[here, half:]
    lower[...] += mxu(right, jnp.concatenate([yh[here, :], yl[here, :], xl[here, half:], right], axis=1), (0, 0))


def pack_upper(out, upper, mirror, turned, f, r):
    half = f // 2
    for i in range(half // B):
        here = pl.ds(i * B, B)
        for j in range(i, f // B):
            b = pl.ds(packed(i, j, f, f + r), B)
            out[:, b] = upper[here, pl.ds(2 * r + f + j * B, B)]
            out[:, b] += upper[here, pl.ds(2 * r + j * B, B)]
            other = upper if j * B < half else mirror
            at = 2 * r if j * B < half else 0
            out[:, b] += other[pl.ds(j * B % half, B), pl.ds(at + i * B, B)].T
        pack_cross(out, i, upper, turned, f, r)


def pack_lower(out, lower, turned, f, r):
    half = f // 2
    for i in range(half // B, f // B):
        here = pl.ds(i * B - half, B)
        for j in range(i, f // B):
            b = pl.ds(packed(i, j, f, f + r), B)
            out[:, b] = lower[here, pl.ds(2 * r + j * B, B)]
            out[:, b] += lower[here, pl.ds(2 * r + j * B - half, B)]
            out[:, b] += lower[pl.ds(j * B - half, B), pl.ds(2 * r + i * B - half, B)].T
        pack_cross(out, i, lower, turned, f, r)


def pack_cross(out, i, acc, turned, f, r):
    here = pl.ds(i * B % (f // 2), B)
    b = pl.ds(packed(i, f // B, f, f + r), r)
    out[:, b] = acc[here, pl.ds(0, r)]
    out[:, b] += acc[here, pl.ds(r, r)]
    out[:, b] += turned[:, pl.ds(i * B, B)].T


def backtest_kernel(
    chunks,
    tile,
    counts_ref,
    codes_ref,
    x_hbm,
    y_hbm,
    out_ref,
    mse_ref,
    xf,
    yf,
    xh,
    xl,
    yh,
    yl,
    upper,
    mirror,
    lower,
    turned,
    part_ref,
    twin_in,
    pair,
    row_in,
    mine,
    z_in,
    before,
    through,
    x_in,
    full,
    system,
    scaled,
    error,
    errors_in,
    loads,
    sends,
    arrivals,
    error_sends,
    error_arrivals,
):
    z, x, r = lax.axis_index("tm_0"), lax.axis_index("tm_1"), lax.axis_index("rows")
    y, core = r // 2, lax.rem(r, 2)
    twin = {"rows": r + 1 - 2 * core}
    count, half, piece = len(chunks), B // 2, B // 8

    def other(i, d):
        return lax.rem(i + d, 4)

    barrier = pltpu.get_barrier_semaphore()
    size = lax.axis_size("rows")
    neighbours = [{"rows": lax.rem(r + d, size)} for d in range(1, size)]
    for d in (1, 2, 3):
        neighbours += [{"tm_0": other(z, d)}, {"tm_1": other(x, d)}]
    for peer in neighbours:
        pl.semaphore_signal(barrier, inc=1, device_id=peer, device_id_type=MESH)
    def load(i):
        here = pl.ds(start_of(i, tile), tile)
        return (
            pltpu.make_async_copy(x_hbm.at[here], xf.at[i % slots], loads.at[2 * i]),
            pltpu.make_async_copy(y_hbm.at[here], yf.at[here], loads.at[2 * i + 1]),
        )

    n, f = xh.shape
    slots = xf.shape[0]
    targets = yf.shape[1]
    tiles = n // tile
    for i in range(slots):
        for copy in load(i):
            copy.start()
    valid_rows = valid_here(counts_ref, n)
    for acc in (upper, mirror, lower, turned):
        acc[...] = jnp.zeros_like(acc)

    def send(phase, j, d, src, dst, peer):
        at = (phase * count + j) * 3 + d - 1
        return pltpu.make_async_remote_copy(
            src_ref=src,
            dst_ref=dst,
            send_sem=sends.at[at],
            recv_sem=arrivals.at[at],
            device_id=peer,
            device_id_type=MESH,
        )

    def multiple(i):
        return pl.multiple_of(i, piece)

    def part(ref, j, start, size, d=None):
        rows = pl.ds(start if isinstance(start, int) else multiple(start), size)
        where = (rows, pl.ds(*chunks[j]))
        return ref.at[where] if d is None else ref.at[(d - 1, *where)]

    def small(ref, j, d=None):
        return part(ref, j, 0, piece, d)

    def to_twin(j):
        return send(0, j, 1, part(part_ref, j, half * (1 - core), half), part(twin_in, j, 0, half), twin)

    def to_row(j, d):
        to = other(y, d)
        return send(1, j, d, part(pair, j, piece * to, piece), small(row_in, j, d), {"rows": 2 * to + core})

    def to_z(j, d):
        return send(2, j, d, small(mine, j), small(z_in, j, d), {"tm_0": other(z, d)})

    def to_x(j, d, src):
        return send(3, j, d, small(src, j), small(x_in, j, d), {"tm_1": other(x, d)})

    def own(j):
        return part(full, j, half * core + piece * y, piece)

    def spread_row(j, d):
        return send(4, j, d, own(j), own(j), {"rows": 2 * other(y, d) + core})

    def row_arrival(j, d):
        there = part(full, j, half * core + piece * other(y, 4 - d), piece)
        return send(4, j, d, there, there, twin)

    def spread_twin(j):
        ours = part(full, j, half * core, half)
        return send(5, j, 1, ours, ours, twin)

    def twin_arrival(j):
        there = part(full, j, half * (1 - core), half)
        return send(5, j, 1, there, there, twin)

    def stage(p, j):
        if p == 0:
            to_twin(j).start()
        if p == 1:
            to_twin(j).wait_recv()
            part(pair, j, 0, half)[...] = (
                part(part_ref, j, half * core, half)[...] + part(twin_in, j, 0, half)[...]
            )
            for d in (1, 2, 3):
                to_row(j, d).start()
        if p == 2:
            total = part(pair, j, piece * y, piece)[...]
            for d in (1, 2, 3):
                to_row(j, d).wait_recv()
                total += small(row_in, j, d)[...]
            small(mine, j)[...] = total
            small(before, j)[...] = jnp.zeros_like(total)
            for d in (1, 2, 3):
                pl.when(z + d < 4)(lambda d=d: to_z(j, d).start())
        if p == 3:
            for d in (1, 2, 3):

                @pl.when(z >= d)
                def _(d=d):
                    to_z(j, d).wait_recv()
                    small(before, j)[...] += small(z_in, j, d)[...]

            small(through, j)[...] = small(before, j)[...] + small(mine, j)[...]
            for d in (1, 2, 3):
                pl.when(x + d < 4)(lambda d=d: to_x(j, d, through).start())
                pl.when(x + d >= 4)(lambda d=d: to_x(j, d, before).start())
        if p == 4:
            total = small(before, j)[...]
            for d in (1, 2, 3):
                to_x(j, d, before).wait_recv()
                total += small(x_in, j, d)[...]
            own(j)[...] = total
            for d in (1, 2, 3):
                spread_row(j, d).start()
        if p == 5:
            for d in (1, 2, 3):
                row_arrival(j, d).wait_recv()
            spread_twin(j).start()
        if p == 6:
            twin_arrival(j).wait_recv()

    def split(i):
        for copy in load(i):
            copy.wait()
        split_tile(i, tile, valid_rows, xf.at[i % slots], yf, xh, xl, yh, yl)

    split(0)

    for i in range(1, tiles):
        if i + slots - 1 < tiles:
            for copy in load(i + slots - 1):
                copy.start()
        upper_products(i - 1, tile, xh, xl, yh, yl, upper, mirror, turned)
        split(i)

    upper_products(tiles - 1, tile, xh, xl, yh, yl, upper, mirror, turned)
    pack_upper(part_ref, upper, mirror, turned, f, targets)
    pl.semaphore_wait(barrier, len(neighbours))
    stage(0, 0)
    early = 2

    @pl.loop(0, early)
    def _(i):
        lower_products(i, tile, xh, xl, yh, yl, lower)

    stage(1, 0)

    @pl.loop(early, tiles)
    def _(i):
        lower_products(i, tile, xh, xl, yh, yl, lower)

    pack_lower(part_ref, lower, turned, f, targets)
    stage(0, 1)
    for p in range(2, 6):
        stage(p, 0)
        stage(p - 1, 1)
    stage(6, 0)

    shard = shard_index()
    seen = jnp.int32(0)
    for k in range(counts_ref.shape[0]):
        seen += jnp.where(k < shard, counts_ref[k], 0)
    first = (shard == 0).astype(F32)
    ridge = codes_ref[jnp.maximum(shard - 1, 0)].astype(F32) * seen.astype(F32) * 0.0625 + first
    columns = f + targets

    def rows_of(k):
        if k == 1:
            stage(5, 1)
        if 2 * k * B == f:
            stage(6, 1)
        return full[:, pl.ds(packed(k, k, f, columns), columns - k * B)]

    solve(rows_of, system, scaled, ridge)
    predict(2 * tile, scaled[:, pl.ds(f, targets)], first - 1.0, valid_rows, xh, xl, yf, out_ref, error)

    errors_in[r] = error[...]

    def send_error(d, slot):
        return pltpu.make_async_remote_copy(
            src_ref=error,
            dst_ref=errors_in.at[slot],
            send_sem=error_sends.at[d - 1],
            recv_sem=error_arrivals.at[d - 1],
            device_id=neighbours[d - 1],
            device_id_type=MESH,
        )

    for d in range(1, size):
        send_error(d, r).start()
    for d in range(1, size):
        send_error(d, lax.rem(r + size - d, size)).wait_recv()
    total = errors_in[0]
    for k in range(1, size):
        total += errors_in[k]
    mse_ref[0] = jnp.sum(total) / (counts_ref[shard].astype(F32) * targets)
    for d in range(1, size):
        send_error(d, r).wait_send()
    for j in range(count):
        to_twin(j).wait_send()
        spread_twin(j).wait_send()
        for d in (1, 2, 3):
            to_row(j, d).wait_send()
            pl.when(z + d < 4)(lambda d=d: to_z(j, d).wait_send())
            to_x(j, d, before).wait_send()
            spread_row(j, d).wait_send()


def backtest(features, targets, counts, codes):
    n, f = features.shape
    r = targets.shape[1]
    half, tile = f // 2, 1024
    first, columns = packed(half // B, half // B, f, f + r), packed(f // B, f // B, f, f + r)
    chunks = [(0, first), (first, columns - first)]
    pair, piece = (B // 2, columns), (B // 8, columns)
    size = lax.axis_size("rows")
    smem, anywhere = pl.BlockSpec(memory_space=pltpu.SMEM), pl.BlockSpec(memory_space=pl.ANY)
    return pl.pallas_call(
        functools.partial(backtest_kernel, chunks, tile),
        in_specs=[smem, smem, anywhere, anywhere],
        out_specs=[pl.BlockSpec(memory_space=pltpu.VMEM), smem],
        out_shape=[jax.ShapeDtypeStruct((n, r), BF), jax.ShapeDtypeStruct((1,), F32)],
        scratch_shapes=[
            pltpu.VMEM((4, tile, f), F32),
            pltpu.VMEM((n, r), F32),
            pltpu.VMEM((n, f), BF),
            pltpu.VMEM((n, f), BF),
            pltpu.VMEM((n, r), BF),
            pltpu.VMEM((n, r), BF),
            pltpu.VMEM((half, 2 * f + 2 * r), F32),
            pltpu.VMEM((half, half), F32),
            pltpu.VMEM((half, f + 2 * r), F32),
            pltpu.VMEM((r, f), F32),
            pltpu.VMEM((B, columns), F32),
            pltpu.VMEM(pair, F32),
            pltpu.VMEM(pair, F32),
            pltpu.VMEM((3, *piece), F32),
            pltpu.VMEM(piece, F32),
            pltpu.VMEM((3, *piece), F32),
            pltpu.VMEM(piece, F32),
            pltpu.VMEM(piece, F32),
            pltpu.VMEM((3, *piece), F32),
            pltpu.VMEM((B, columns), F32),
            pltpu.VMEM((f, f + r), F32),
            pltpu.VMEM((f, f + r), F32),
            pltpu.VMEM((8, r), F32),
            pltpu.VMEM((size, 8, r), F32),
            pltpu.SemaphoreType.DMA((2 * n // tile,)),
            pltpu.SemaphoreType.DMA((18 * len(chunks),)),
            pltpu.SemaphoreType.DMA((18 * len(chunks),)),
            pltpu.SemaphoreType.DMA((size - 1,)),
            pltpu.SemaphoreType.DMA((size - 1,)),
        ],
        compiler_params=pltpu.CompilerParams(
            collective_id=0, has_side_effects=True, vmem_limit_bytes=51 * 2**20
        ),
        name="backtest",
    )(counts, codes, features, targets)


def body(features, targets, row_counts, ridge_codes):
    return tuple(backtest(features, targets, row_counts, ridge_codes))


def solution(mesh):
    finer = Mesh(mesh.devices.reshape(4, 4, mesh.shape["rows"]), ("tm_0", "tm_1", "rows"))
    placed = (P(TM_ROWS, None), P(TM_ROWS, None), P(), P())
    return jax.shard_map(
        body, mesh=finer, in_specs=placed, out_specs=(P(TM_ROWS, None), P(TM)), check_vma=False
    )
```

```python
import functools

import jax
import jax.numpy as jnp
from jax import lax
from jax.experimental import pallas as pl
from jax.experimental.pallas import tpu as pltpu
from jax.sharding import Mesh
from jax.sharding import PartitionSpec as P

TM = ("tm_0", "tm_1")
TM_ROWS = ("tm_0", "tm_1", "rows")
F32 = jnp.float32
BF = jnp.bfloat16
B = 128
WIDE = 16
MESH = pl.DeviceIdType.MESH


def halves_of(x):
    high = x.astype(BF)
    return high, (x - high.astype(F32)).astype(BF)


def thirds_of(x):
    high = x.astype(BF)
    left = x - high.astype(F32)
    middle = left.astype(BF)
    return high, middle, (left - middle.astype(F32)).astype(BF)


def mxu(left, right, dims=(1, 0)):
    contract = (((dims[0],), (dims[1],)), ((), ()))
    return lax.dot_general(left, right, contract, preferred_element_type=F32)


def packed(i, j, f, width):
    return sum(width - k * B for k in range(i)) + (j - i) * B


def full_dot(a, b, dims=(1, 0)):
    ah, am, al = thirds_of(a)
    bh, bm, bl = thirds_of(b)
    left = jnp.concatenate([ah, ah, am, am, ah, al], axis=dims[0])
    right = jnp.concatenate([bh, bm, bh, bm, bl, bh], axis=dims[1])
    return mxu(left, right, dims)


def shard_index():
    return lax.axis_index("tm_0") * lax.axis_size("tm_1") + lax.axis_index("tm_1")


def valid_here(counts_ref, rows):
    return counts_ref[shard_index()] - lax.axis_index("rows") * rows


def row_of(x, s):
    return jnp.take_along_axis(x, jnp.full((8, B), s, jnp.int32), axis=0)


def column_of(x, c):
    return jnp.broadcast_to(x[:, c : c + 1], (8, B))


def negative_inverse(block):
    block = list(block)
    sub = lax.broadcasted_iota(jnp.int32, (8, B), 0)
    lane = lax.broadcasted_iota(jnp.int32, (8, B), 1)
    halves = WIDE // 8
    steps = B // WIDE
    for g in range(steps):
        mine = [halves * g + h for h in range(halves)]
        ahead = [halves * (g + 1) + h for h in range(halves)] if g + 1 < steps else []
        lo = WIDE * g
        inside = (lane >= lo) & (lane < lo + WIDE)
        cols = [[column_of(block[m], lo + c) for m in mine] for c in range(WIDE)]
        rows = jnp.concatenate([block[m] for m in mine], axis=0)
        right = [
            jnp.where(inside, jnp.where(lane - lo - 8 * h == sub, -1.0, 0.0), block[m])
            for h, m in enumerate(mine)
        ]
        later = {j: [column_of(block[j], lo + c) for c in range(WIDE)] for j in ahead}
        for p in range(WIDE // 2):
            r0, r1 = 2 * p, 2 * p + 1
            h, s0, s1 = r0 // 8, r0 % 8, r0 % 8 + 1
            a, b, c = row_of(cols[r0][h], s0), row_of(cols[r1][h], s0), row_of(cols[r1][h], s1)
            inverse = pl.reciprocal(a * c - b * b)
            at0, at1 = sub == s0, sub == s1
            both = at0 | at1
            n0, n1 = [], []
            for k in range(halves):
                x0 = cols[r0][k] * c - cols[r1][k] * b
                x1 = cols[r1][k] * a - cols[r0][k] * b
                if k == h:
                    x0 = jnp.where(at0, -c, jnp.where(at1, b, x0))
                    x1 = jnp.where(at0, b, jnp.where(at1, -a, x1))
                n0.append(x0)
                n1.append(x1)

            def swept(column):
                u, v = row_of(column[h], s0), row_of(column[h], s1)
                out = []
                for k in range(halves):
                    old = jnp.where(both, 0.0, column[k]) if k == h else column[k]
                    out.append(old - (n0[k] * u + n1[k] * v) * inverse)
                return out

            for q in range(r1 + 1, WIDE):
                cols[q] = swept(cols[q])
            right = swept(right)
        outer = full_dot(rows, jnp.concatenate(right, axis=0), (0, 0))
        terms = [row_of(right[c // 8], c % 8) for c in range(WIDE)] if ahead else None
        for j in range(B // 8):
            if j in mine:
                block[j] = right[j - mine[0]]
            elif j in ahead:
                value = jnp.where(inside, 0.0, block[j])
                for c in range(WIDE):
                    value = value - later[j][c] * terms[c]
                block[j] = value
            else:
                block[j] = jnp.where(inside, 0.0, block[j]) - outer[8 * j : 8 * j + 8, :]
    return jnp.concatenate(block, axis=0)


def solve(rows_of, system, scaled, ridge):
    f, width = system.shape
    count = f // B
    diagonal = lax.broadcasted_iota(jnp.int32, (B, B), 0) == lax.broadcasted_iota(jnp.int32, (B, B), 1)
    for k in range(count):
        here, part = pl.ds(k * B, B), pl.ds(k * B, width - k * B)
        system[here, part] = rows_of(k)
        if k:
            earlier = pl.ds(0, k * B)
            system[here, part] += full_dot(system[earlier, here], scaled[earlier, part], (0, 0))
        block = system[here, here] + jnp.where(diagonal, ridge, 0.0)
        inverse = negative_inverse([block[8 * i : 8 * i + 8, :] for i in range(B // 8)])
        rest = pl.ds((k + 1) * B, width - (k + 1) * B)
        scaled[here, rest] = full_dot(inverse, system[here, rest])
    last = pl.ds(f, width - f)
    for j in range(count - 2, -1, -1):
        here, behind = pl.ds(j * B, B), pl.ds((j + 1) * B, f - (j + 1) * B)
        scaled[here, last] += full_dot(scaled[here, behind], scaled[behind, last])


def predict(tile, solution_part, scale, valid_rows, xh, xl, y, out_ref, error):
    n, r = y.shape
    wh, wl = halves_of(solution_part * scale)
    both = jnp.concatenate([wh, wl], axis=1)
    error[...] = jnp.zeros_like(error)

    for i in range(n // tile):
        here = pl.ds(start_of(i, tile), tile)
        first = mxu(xh[here, :], both)
        value = first[:, :r] + first[:, r:] + mxu(xl[here, :], wh)
        out_ref[here, :] = value.astype(BF)
        valid = i * tile + lax.broadcasted_iota(jnp.int32, (tile, r), 0) < valid_rows
        gap = jnp.where(valid, y[here, :] - value, 0.0)
        error[...] += jnp.sum((gap * gap).reshape(tile // 8, 8, r), axis=0)


def start_of(i, tile):
    return i * tile if isinstance(i, int) else pl.multiple_of(i * tile, tile)


def split_tile(i, tile, valid_rows, x, y, xh, xl, yh, yl):
    here = pl.ds(start_of(i, tile), tile)
    valid = i * tile + lax.broadcasted_iota(jnp.int32, (tile, 1), 0) < valid_rows
    xh[here, :], xl[here, :] = halves_of(jnp.where(valid, x[...], 0.0))
    yh[here, :], yl[here, :] = halves_of(y[here, :])


def upper_products(i, tile, xh, xl, yh, yl, upper, mirror, turned):
    here = pl.ds(start_of(i, tile), tile)
    half = xh.shape[1] // 2
    left, right = xh[here, :half], xh[here, half:]
    low = xl[here, :]
    high = yh[here, :]
    upper[...] += mxu(left, jnp.concatenate([high, yl[here, :], low, left, right], axis=1), (0, 0))
    mirror[...] += mxu(right, low[:, :half], (0, 0))
    turned[...] += mxu(high, low, (0, 0))


def lower_products(i, tile, xh, xl, yh, yl, lower):
    here = pl.ds(start_of(i, tile), tile)
    half = xh.shape[1] // 2
    right = xh[here, half:]
    lower[...] += mxu(right, jnp.concatenate([yh[here, :], yl[here, :], xl[here, half:], right], axis=1), (0, 0))


def pack_upper(out, upper, mirror, turned, f, r):
    half = f // 2
    for i in range(half // B):
        here = pl.ds(i * B, B)
        for j in range(i, f // B):
            b = pl.ds(packed(i, j, f, f + r), B)
            out[:, b] = upper[here, pl.ds(2 * r + f + j * B, B)]
            out[:, b] += upper[here, pl.ds(2 * r + j * B, B)]
            other = upper if j * B < half else mirror
            at = 2 * r if j * B < half else 0
            out[:, b] += other[pl.ds(j * B % half, B), pl.ds(at + i * B, B)].T
        pack_cross(out, i, upper, turned, f, r)


def pack_lower(out, lower, turned, f, r):
    half = f // 2
    for i in range(half // B, f // B):
        here = pl.ds(i * B - half, B)
        for j in range(i, f // B):
            b = pl.ds(packed(i, j, f, f + r), B)
            out[:, b] = lower[here, pl.ds(2 * r + j * B, B)]
            out[:, b] += lower[here, pl.ds(2 * r + j * B - half, B)]
            out[:, b] += lower[pl.ds(j * B - half, B), pl.ds(2 * r + i * B - half, B)].T
        pack_cross(out, i, lower, turned, f, r)


def pack_cross(out, i, acc, turned, f, r):
    here = pl.ds(i * B % (f // 2), B)
    b = pl.ds(packed(i, f // B, f, f + r), r)
    out[:, b] = acc[here, pl.ds(0, r)]
    out[:, b] += acc[here, pl.ds(r, r)]
    out[:, b] += turned[:, pl.ds(i * B, B)].T


def backtest_kernel(
    chunks,
    tile,
    counts_ref,
    codes_ref,
    x_hbm,
    y_hbm,
    out_ref,
    mse_ref,
    xf,
    yf,
    xh,
    xl,
    yh,
    yl,
    upper,
    mirror,
    lower,
    turned,
    part_ref,
    twin_in,
    pair,
    row_in,
    mine,
    z_in,
    before,
    through,
    x_in,
    full,
    system,
    scaled,
    error,
    errors_in,
    loads,
    sends,
    arrivals,
    error_sends,
    error_arrivals,
):
    z, x, r = lax.axis_index("tm_0"), lax.axis_index("tm_1"), lax.axis_index("rows")
    y, core = r // 2, lax.rem(r, 2)
    twin = {"rows": r + 1 - 2 * core}
    count, half, piece = len(chunks), B // 2, B // 8

    def other(i, d):
        return lax.rem(i + d, 4)

    barrier = pltpu.get_barrier_semaphore()
    size = lax.axis_size("rows")
    neighbours = [{"rows": lax.rem(r + d, size)} for d in range(1, size)]
    for d in (1, 2, 3):
        neighbours += [{"tm_0": other(z, d)}, {"tm_1": other(x, d)}]
    for peer in neighbours:
        pl.semaphore_signal(barrier, inc=1, device_id=peer, device_id_type=MESH)
    def load(i):
        here = pl.ds(start_of(i, tile), tile)
        return (
            pltpu.make_async_copy(x_hbm.at[here], xf.at[i % slots], loads.at[2 * i]),
            pltpu.make_async_copy(y_hbm.at[here], yf.at[here], loads.at[2 * i + 1]),
        )

    n, f = xh.shape
    slots = xf.shape[0]
    targets = yf.shape[1]
    tiles = n // tile
    for i in range(slots):
        for copy in load(i):
            copy.start()
    valid_rows = valid_here(counts_ref, n)
    for acc in (upper, mirror, lower, turned):
        acc[...] = jnp.zeros_like(acc)

    def send(phase, j, d, src, dst, peer):
        at = (phase * count + j) * 3 + d - 1
        return pltpu.make_async_remote_copy(
            src_ref=src,
            dst_ref=dst,
            send_sem=sends.at[at],
            recv_sem=arrivals.at[at],
            device_id=peer,
            device_id_type=MESH,
        )

    def multiple(i):
        return pl.multiple_of(i, piece)

    def part(ref, j, start, size, d=None):
        rows = pl.ds(start if isinstance(start, int) else multiple(start), size)
        where = (rows, pl.ds(*chunks[j]))
        return ref.at[where] if d is None else ref.at[(d - 1, *where)]

    def small(ref, j, d=None):
        return part(ref, j, 0, piece, d)

    def to_twin(j):
        return send(0, j, 1, part(part_ref, j, half * (1 - core), half), part(twin_in, j, 0, half), twin)

    def to_row(j, d):
        to = other(y, d)
        return send(1, j, d, part(pair, j, piece * to, piece), small(row_in, j, d), {"rows": 2 * to + core})

    def to_z(j, d):
        return send(2, j, d, small(mine, j), small(z_in, j, d), {"tm_0": other(z, d)})

    def to_x(j, d, src):
        return send(3, j, d, small(src, j), small(x_in, j, d), {"tm_1": other(x, d)})

    def own(j):
        return part(full, j, half * core + piece * y, piece)

    def spread_row(j, d):
        return send(4, j, d, own(j), own(j), {"rows": 2 * other(y, d) + core})

    def row_arrival(j, d):
        there = part(full, j, half * core + piece * other(y, 4 - d), piece)
        return send(4, j, d, there, there, twin)

    def spread_twin(j):
        ours = part(full, j, half * core, half)
        return send(5, j, 1, ours, ours, twin)

    def twin_arrival(j):
        there = part(full, j, half * (1 - core), half)
        return send(5, j, 1, there, there, twin)

    def stage(p, j):
        if p == 0:
            to_twin(j).start()
        if p == 1:
            to_twin(j).wait_recv()
            part(pair, j, 0, half)[...] = (
                part(part_ref, j, half * core, half)[...] + part(twin_in, j, 0, half)[...]
            )
            for d in (1, 2, 3):
                to_row(j, d).start()
        if p == 2:
            total = part(pair, j, piece * y, piece)[...]
            for d in (1, 2, 3):
                to_row(j, d).wait_recv()
                total += small(row_in, j, d)[...]
            small(mine, j)[...] = total
            small(before, j)[...] = jnp.zeros_like(total)
            for d in (1, 2, 3):
                pl.when(z + d < 4)(lambda d=d: to_z(j, d).start())
        if p == 3:
            for d in (1, 2, 3):

                @pl.when(z >= d)
                def _(d=d):
                    to_z(j, d).wait_recv()
                    small(before, j)[...] += small(z_in, j, d)[...]

            small(through, j)[...] = small(before, j)[...] + small(mine, j)[...]
            for d in (1, 2, 3):
                pl.when(x + d < 4)(lambda d=d: to_x(j, d, through).start())
                pl.when(x + d >= 4)(lambda d=d: to_x(j, d, before).start())
        if p == 4:
            total = small(before, j)[...]
            for d in (1, 2, 3):
                to_x(j, d, before).wait_recv()
                total += small(x_in, j, d)[...]
            own(j)[...] = total
            for d in (1, 2, 3):
                spread_row(j, d).start()
        if p == 5:
            for d in (1, 2, 3):
                row_arrival(j, d).wait_recv()
            spread_twin(j).start()
        if p == 6:
            twin_arrival(j).wait_recv()

    def split(i):
        for copy in load(i):
            copy.wait()
        split_tile(i, tile, valid_rows, xf.at[i % slots], yf, xh, xl, yh, yl)

    split(0)

    for i in range(1, tiles):
        if i + slots - 1 < tiles:
            for copy in load(i + slots - 1):
                copy.start()
        upper_products(i - 1, tile, xh, xl, yh, yl, upper, mirror, turned)
        split(i)

    upper_products(tiles - 1, tile, xh, xl, yh, yl, upper, mirror, turned)
    pack_upper(part_ref, upper, mirror, turned, f, targets)
    pl.semaphore_wait(barrier, len(neighbours))
    stage(0, 0)
    early = 2

    for i in range(0, early):
        lower_products(i, tile, xh, xl, yh, yl, lower)

    stage(1, 0)

    for i in range(early, tiles):
        lower_products(i, tile, xh, xl, yh, yl, lower)

    pack_lower(part_ref, lower, turned, f, targets)
    stage(0, 1)
    for p in range(2, 6):
        stage(p, 0)
        stage(p - 1, 1)
    stage(6, 0)

    shard = shard_index()
    seen = jnp.int32(0)
    for k in range(counts_ref.shape[0]):
        seen += jnp.where(k < shard, counts_ref[k], 0)
    first = (shard == 0).astype(F32)
    ridge = codes_ref[jnp.maximum(shard - 1, 0)].astype(F32) * seen.astype(F32) * 0.0625 + first
    columns = f + targets

    def rows_of(k):
        if k == 1:
            stage(5, 1)
        if 2 * k * B == f:
            stage(6, 1)
        return full[:, pl.ds(packed(k, k, f, columns), columns - k * B)]

    solve(rows_of, system, scaled, ridge)
    predict(2 * tile, scaled[:, pl.ds(f, targets)], first - 1.0, valid_rows, xh, xl, yf, out_ref, error)

    errors_in[r] = error[...]

    def send_error(d, slot):
        return pltpu.make_async_remote_copy(
            src_ref=error,
            dst_ref=errors_in.at[slot],
            send_sem=error_sends.at[d - 1],
            recv_sem=error_arrivals.at[d - 1],
            device_id=neighbours[d - 1],
            device_id_type=MESH,
        )

    for d in range(1, size):
        send_error(d, r).start()
    for d in range(1, size):
        send_error(d, lax.rem(r + size - d, size)).wait_recv()
    total = errors_in[0]
    for k in range(1, size):
        total += errors_in[k]
    mse_ref[0] = jnp.sum(total) / (counts_ref[shard].astype(F32) * targets)
    for d in range(1, size):
        send_error(d, r).wait_send()
    for j in range(count):
        to_twin(j).wait_send()
        spread_twin(j).wait_send()
        for d in (1, 2, 3):
            to_row(j, d).wait_send()
            pl.when(z + d < 4)(lambda d=d: to_z(j, d).wait_send())
            to_x(j, d, before).wait_send()
            spread_row(j, d).wait_send()


def backtest(features, targets, counts, codes):
    n, f = features.shape
    r = targets.shape[1]
    half, tile = f // 2, 1024
    first, columns = packed(half // B, half // B, f, f + r), packed(f // B, f // B, f, f + r)
    chunks = [(0, first), (first, columns - first)]
    pair, piece = (B // 2, columns), (B // 8, columns)
    size = lax.axis_size("rows")
    smem, anywhere = pl.BlockSpec(memory_space=pltpu.SMEM), pl.BlockSpec(memory_space=pl.ANY)
    return pl.pallas_call(
        functools.partial(backtest_kernel, chunks, tile),
        in_specs=[smem, smem, anywhere, anywhere],
        out_specs=[pl.BlockSpec(memory_space=pltpu.VMEM), smem],
        out_shape=[jax.ShapeDtypeStruct((n, r), BF), jax.ShapeDtypeStruct((1,), F32)],
        scratch_shapes=[
            pltpu.VMEM((4, tile, f), F32),
            pltpu.VMEM((n, r), F32),
            pltpu.VMEM((n, f), BF),
            pltpu.VMEM((n, f), BF),
            pltpu.VMEM((n, r), BF),
            pltpu.VMEM((n, r), BF),
            pltpu.VMEM((half, 2 * f + 2 * r), F32),
            pltpu.VMEM((half, half), F32),
            pltpu.VMEM((half, f + 2 * r), F32),
            pltpu.VMEM((r, f), F32),
            pltpu.VMEM((B, columns), F32),
            pltpu.VMEM(pair, F32),
            pltpu.VMEM(pair, F32),
            pltpu.VMEM((3, *piece), F32),
            pltpu.VMEM(piece, F32),
            pltpu.VMEM((3, *piece), F32),
            pltpu.VMEM(piece, F32),
            pltpu.VMEM(piece, F32),
            pltpu.VMEM((3, *piece), F32),
            pltpu.VMEM((B, columns), F32),
            pltpu.VMEM((f, f + r), F32),
            pltpu.VMEM((f, f + r), F32),
            pltpu.VMEM((8, r), F32),
            pltpu.VMEM((size, 8, r), F32),
            pltpu.SemaphoreType.DMA((2 * n // tile,)),
            pltpu.SemaphoreType.DMA((18 * len(chunks),)),
            pltpu.SemaphoreType.DMA((18 * len(chunks),)),
            pltpu.SemaphoreType.DMA((size - 1,)),
            pltpu.SemaphoreType.DMA((size - 1,)),
        ],
        compiler_params=pltpu.CompilerParams(
            collective_id=0, has_side_effects=True, vmem_limit_bytes=51 * 2**20
        ),
        name="backtest",
    )(counts, codes, features, targets)


def body(features, targets, row_counts, ridge_codes):
    return tuple(backtest(features, targets, row_counts, ridge_codes))


def solution(mesh):
    finer = Mesh(mesh.devices.reshape(4, 4, mesh.shape["rows"]), ("tm_0", "tm_1", "rows"))
    placed = (P(TM_ROWS, None), P(TM_ROWS, None), P(), P())
    return jax.shard_map(
        body, mesh=finer, in_specs=placed, out_specs=(P(TM_ROWS, None), P(TM)), check_vma=False
    )
```
